32 devices in a mesh: modes: 2 (over x), space: 16 (over z, y, core).
Axes of the slice: x: 2, y: 2, z: 4, core: 2. Of those that a mesh axis runs over, the one named last changes fastest.
Arguments:
- mode_coeffs: float32 [120, 16, 120, 128], P('modes', 'space'), may hold values from -6 to 6
- mean_perm: float32 [16, 120, 128], P('space'), may hold values from 0.5 to 2
- kl_fields: float32 [7, 16, 120, 128], P(None, 'space'), may hold values from -4 to 4
- couplings: float32 [7, 120, 120], replicated, may hold values from -0.5 to 0.5
Outputs:
- applied: float32 [120, 16, 120, 128], P('modes', 'space')
The draws below stay inside these ranges and needn't reach their ends.
All inputs are finite; a program needn't handle non-finite values.
Results may differ from the reference program's by a relative error of at most 0.0001.
Values sent between devices are 32-bit elements; how exact they have to be, the bound alone decides.
No kernel may reach another device: no remote copies, remote signals or barrier semaphores. Data moves between devices by JAX's collectives and lax.ppermute only.
A program may use at most 448 MiB of HBM per device.

```python
import math
import jax
import jax.numpy as jnp
from jax import lax

MODES = 120
KL = 7
NY = 120
NZ = 128
NX = 16


def level_of(stream_key, dims, cuts, low, high):
    loudness, own = 1.0, jax.random.fold_in(stream_key, 6)
    for axis_at, blocks in cuts:
        heights = jnp.exp(jax.random.uniform(jax.random.fold_in(own, axis_at), (blocks,), jnp.float32, low / len(cuts), high / len(cuts)))
        loudness = loudness * jnp.repeat(heights, dims[axis_at] // blocks).reshape([-1 if axis == axis_at else 1 for axis in range(len(dims))])
    return loudness


def normal_values(own_key, dims, scale, bound, cuts=(), kind=jnp.bfloat16):
    factor_of = level_of(own_key, dims, cuts, -0.22, 0.18) if cuts else 1.0
    values = jax.random.normal(own_key, dims, jnp.float32) * scale * factor_of
    return jnp.minimum(jnp.maximum(values, -bound), bound).astype(kind)


def setup_inputs(seed: int = 0) -> dict:
    seeds = jax.random.split(jax.random.key(seed), 5)
    return {
        "mode_coeffs": normal_values(seeds[0], (MODES, NX, NY, NZ), 1.0, 6.0, ((0, 2), (1, 16)), jnp.float32),
        "mean_perm": jnp.clip(jnp.exp(math.log(2.0) - 1.3862944 * jax.random.uniform(seeds[1], (NX, NY, NZ), jnp.float32) ** level_of(seeds[1], (NX, NY, NZ), ((0, 16),), -0.2, 0.2)), 0.5, 2.0),
        "kl_fields": normal_values(seeds[2], (KL, NX, NY, NZ), 0.3, 4.0, ((1, 16),), jnp.float32),
        "couplings": normal_values(seeds[3], (KL, MODES, MODES), MODES ** -0.5, 0.5, (), jnp.float32),
    }


def shifted(padded, direction, offset):
    result = padded
    base = padded.ndim - 3
    for axis_index in range(3):
        extent = padded.shape[base + axis_index] - 2
        begin = offset if axis_index == direction else 1
        result = lax.slice_in_dim(result, begin, begin + extent, axis=base + axis_index)
    return result


def operate(field_pad, perm_pad):
    centre = shifted(field_pad, 0, 1)
    centre_perm = shifted(perm_pad, 0, 1)
    terms = []
    for direction in range(3):
        for offset in (0, 2):
            face_perm = 0.5 * (centre_perm + shifted(perm_pad, direction, offset))
            terms.append(face_perm * (centre - shifted(field_pad, direction, offset)))
    accum_total = terms[0]
    for extra_term in terms[1:]:
        accum_total = accum_total + extra_term
    return accum_total


def pad_cells(source):
    widths = [(0, 0)] * (source.ndim - 3) + [(1, 1)] * 3
    return jnp.pad(source, widths)


def reference(mode_coeffs, mean_perm, kl_fields, couplings):
    flat_modes = mode_coeffs.reshape(mode_coeffs.shape[0], -1)
    result = operate(pad_cells(mode_coeffs), pad_cells(mean_perm))
    for term_index in range(KL):
        mixed_modes = jnp.dot(couplings[term_index], flat_modes, precision=lax.Precision.HIGHEST).reshape(mode_coeffs.shape)
        result = result + operate(pad_cells(mixed_modes), pad_cells(kl_fields[term_index]))
    return result
```

```python
import functools

import jax
import jax.numpy as jnp
from jax import lax
from jax.experimental import pallas as pl
from jax.experimental.pallas import tpu as pltpu
from jax.sharding import PartitionSpec as P

SUB = 8
PACK = 16
FACES = 6
LIMIT = 48 * 2**20
VMEM = pl.BlockSpec(memory_space=pltpu.VMEM)


def halves(value):
    high = value.astype(jnp.bfloat16)
    low = (value - high.astype(jnp.float32)).astype(jnp.bfloat16)
    return high, low


def face_coefs(coef, perm, perm_up, perm_down, begin, count):
    terms = perm.shape[0]
    lane = lax.broadcasted_iota(jnp.int32, (count, perm.shape[2]), 1)
    width = perm.shape[2]
    for k in range(terms):
        here = perm[k, pl.ds(begin + SUB, count), :]
        others = (
            perm_up[k, pl.ds(begin + SUB, count), :],
            perm_down[k, pl.ds(begin + SUB, count), :],
            perm[k, pl.ds(begin + SUB + 1, count), :],
            perm[k, pl.ds(begin + SUB - 1, count), :],
            jnp.where(lane < width - 1, pltpu.roll(here, width - 1, 1), 0.0),
            jnp.where(lane > 0, pltpu.roll(here, 1, 1), 0.0),
        )
        for f, other in enumerate(others):
            coef[f * terms + k, pl.ds(0, count), :] = 0.5 * (here + other)


def strided_rows(ref, start, count, stride):
    return ref[pl.ds(start, count, stride=stride), :]


def gathered_kernel(first, count, rows, mode_dev, pad, groups, sources, *refs):
    own, perm, perm_up, perm_down, weights = refs[:5]
    pieces = refs[5 : 5 + len(sources) * (groups - 1)]
    out, to_up, to_down = refs[5 + len(pieces) : 8 + len(pieces)]
    coef, cells, stack, mixed, pending, above = refs[8 + len(pieces) :]
    terms = perm.shape[0]
    nz = own.shape[1]
    low_row, last = max(first - 1, 0), min(first + count, rows - 1)
    face_coefs(coef, perm, perm_up, perm_down, low_row, last - low_row + 1)
    cells[...] = jnp.zeros_like(cells)
    pending[...] = jnp.zeros_like(pending)
    above[...] = jnp.zeros_like(above)
    lane = lax.broadcasted_iota(jnp.int32, (SUB, nz), 1)
    wide = groups * pad

    def fill(slot, row, source):
        lanes = pl.ds(slot * nz, nz)
        start, length, at = source
        cells[slot, 0, :mode_dev, :] = strided_rows(own, row, mode_dev, rows)
        for s in range(1, groups):
            piece = pieces[at * (groups - 1) + s - 1]
            cells[slot, s, :mode_dev, :] = strided_rows(piece, row - start, mode_dev, length)
        high, low = halves(cells[slot].reshape(wide, nz))
        stack[0:wide, lanes] = high
        stack[wide : 2 * wide, lanes] = low
        stack[2 * wide : 3 * wide, lanes] = high

    def finish(row, block, value):
        size = min(SUB, mode_dev - block * SUB)
        out[pl.ds(block * SUB * count + row - first, size, stride=count), :] = value[:size]

    def spread(slot, row):
        lanes = pl.ds(slot * nz, nz)
        local_row = row - low_row
        factors = [
            [jnp.broadcast_to(coef[f * terms + k, pl.ds(local_row, 1), :], (SUB, nz)) for k in range(terms)]
            for f in range(FACES)
        ]
        inside = jnp.logical_and(row >= first, row < first + count)
        for block in range(pl.cdiv(mode_dev, SUB)):
            size = min(SUB, mode_dev - block * SUB)
            here = pl.ds(block * SUB, SUB)
            totals = [None] * FACES
            for k in range(terms):
                if k == terms - 1:
                    value = cells[slot, 0, here, :]
                else:
                    value = mixed[pl.ds(k * pad + block * SUB, SUB), lanes]
                for f in range(FACES):
                    part = factors[f][k] * value
                    totals[f] = part if totals[f] is None else totals[f] + part
            up, down, north, south, east, west = totals
            before = pending[here, :] - south

            @pl.when(row > first)
            def _():
                finish(row - 1, block, before)

            @pl.when(inside)
            def _():
                at = pl.ds(block * SUB * count + row - first, size, stride=count)
                to_up[at, :] = -up[:size]
                to_down[at, :] = -down[:size]

            moved_east = jnp.where(lane > 0, pltpu.roll(east, 1, 1), 0.0)
            moved_west = jnp.where(lane < nz - 1, pltpu.roll(west, nz - 1, 1), 0.0)
            total = ((up + down) + (north + south)) + ((east - moved_east) + (west - moved_west))
            pending[here, :] = total - above[here, :]
            above[here, :] = north

    def process(row, number, source):
        for slot in range(number):
            fill(slot, row + slot, source)
        span = number * nz
        mixed[:, 0:span] = jnp.dot(
            weights[...], stack[:, 0:span], preferred_element_type=jnp.float32
        )
        for slot in range(number):
            spread(slot, row + slot)

    at_row = low_row
    for index, (start, length) in enumerate(sources):
        source = (start, length, index)
        end = min(start + length, last + 1)
        pairs = (end - at_row) // 2

        def body(step, carry, source=source, base=at_row):
            process(base + 2 * step, 2, source)
            return carry

        lax.fori_loop(0, pairs, body, 0)
        if (end - at_row) % 2:
            process(jnp.int32(end - 1), 1, source)
        at_row = end
    if first + count == rows:
        for block in range(pl.cdiv(mode_dev, SUB)):
            finish(rows - 1, block, pending[pl.ds(block * SUB, SUB), :])


def partial_kernel(first, count, rows, mode_dev, pad, groups, *refs):
    own, up, down, perm, perm_up, perm_down, weights, out = refs[:8]
    sends = refs[8 : 8 + groups - 1]
    coef, near, high, low = refs[8 + groups - 1 :]
    terms = perm.shape[0]
    nz = own.shape[1]
    face_coefs(coef, perm, perm_up, perm_down, first, count)
    near[...] = jnp.zeros_like(near)
    lane = lax.broadcasted_iota(jnp.int32, (PACK, nz), 1)
    wide = groups * pad

    def process(row, number):
        for slot in range(number + 2):
            at = row + slot - 1
            value = strided_rows(own, jnp.clip(at, 0, rows - 1), mode_dev, rows)
            near[slot, :mode_dev, :] = jnp.where(jnp.logical_and(at >= 0, at < rows), value, 0.0)
        mean_parts = []
        for slot in range(number):
            lanes = pl.ds(slot * nz, nz)
            local_row = row + slot - first
            near[4, :mode_dev, :] = strided_rows(up, local_row, mode_dev, count)
            near[5, :mode_dev, :] = strided_rows(down, local_row, mode_dev, count)
            factors = [
                [jnp.broadcast_to(coef[f * terms + k, pl.ds(local_row, 1), :], (SUB, nz)) for k in range(terms)]
                for f in range(FACES)
            ]
            factors = [[jnp.concatenate([x, x], 0) for x in line] for line in factors]
            blocks = []
            for block in range(pad // PACK):
                here = pl.ds(block * PACK, PACK)
                centre = near[slot + 1, here, :]
                others = (
                    near[4, here, :],
                    near[5, here, :],
                    near[slot + 2, here, :],
                    near[slot, here, :],
                    jnp.where(lane < nz - 1, pltpu.roll(centre, nz - 1, 1), 0.0),
                    jnp.where(lane > 0, pltpu.roll(centre, 1, 1), 0.0),
                )
                steps = [centre - other for other in others]
                for k in range(terms):
                    total = factors[0][k] * steps[0]
                    for f in range(1, FACES):
                        total = total + factors[f][k] * steps[f]
                    if k == terms - 1:
                        blocks.append(total)
                    else:
                        place = pl.ds(k * pad + block * PACK, PACK)
                        high[place, lanes], low[place, lanes] = halves(total)
            mean_parts.append(blocks)
        span = number * nz
        both = jnp.dot(weights[...], high[:, 0:span], preferred_element_type=jnp.float32)
        rest = jnp.dot(weights[0:wide, :], low[:, 0:span], preferred_element_type=jnp.float32)
        result = both[0:wide] + both[wide : 2 * wide] + rest
        for slot in range(number):
            local_row = row + slot - first
            lanes = slice(slot * nz, (slot + 1) * nz)
            mean_part = jnp.concatenate(mean_parts[slot], 0)
            for s in range(groups):
                target = out if s == 0 else sends[s - 1]
                value = result[s * pad : (s + 1) * pad, lanes]
                if s == 0:
                    value = value + mean_part
                target[pl.ds(local_row, mode_dev, stride=count), :] = value[:mode_dev]

    def body(step, carry):
        process(first + 2 * step, 2)
        return carry

    lax.fori_loop(0, count // 2, body, 0)


def sum_kernel(*refs):
    *parts, out = refs
    total = parts[0][...]
    for part in parts[1:]:
        total = total + part[...]
    out[...] = total


def place_sum(result, parts, first, shape):
    modes, count, nz = parts[0].shape
    kept = [] if result is None else [result]

    def kernel(*refs):
        sum_kernel(*refs[len(kept) :])

    return pl.pallas_call(
        kernel,
        grid=(count // SUB,),
        in_specs=[pl.BlockSpec(memory_space=pl.ANY)] * len(kept)
        + [pl.BlockSpec((modes, SUB, nz), lambda i: (0, i, 0))] * len(parts),
        out_specs=pl.BlockSpec((modes, SUB, nz), lambda i: (0, i + first // SUB, 0)),
        out_shape=jax.ShapeDtypeStruct(shape, jnp.float32),
        input_output_aliases={0: 0} if kept else {},
    )(*kept, *parts)


def local(mode_coeffs, mean_perm, kl_fields, couplings):
    mode_dev, _, rows, nz = mode_coeffs.shape
    terms = kl_fields.shape[0] + 1
    groups = lax.axis_size("modes")
    planes = lax.axis_size("space")
    pad = pl.cdiv(mode_dev, PACK) * PACK
    group = lax.axis_index("modes")
    forward = [(i, i + 1) for i in range(planes - 1)]
    backward = [(target, source) for source, target in forward]
    own3 = mode_coeffs.reshape(mode_dev, rows, nz)
    own = own3.reshape(mode_dev * rows, nz)

    def rotated(value, step):
        return lax.ppermute(value, "modes", [(i, (i + step) % groups) for i in range(groups)])

    def widened(value):
        return jnp.pad(value, ((0, 0), (SUB, SUB), (0, 0)))

    def block(row_group, column_group):
        piece = lax.dynamic_slice(
            couplings,
            (0, (row_group % groups) * mode_dev, (column_group % groups) * mode_dev),
            (terms - 1, mode_dev, mode_dev),
        )
        return jnp.pad(piece, ((0, 0), (0, pad - mode_dev), (0, pad - mode_dev)))

    def split(value):
        high = lax.reduce_precision(value, 8, 7)
        return high.astype(jnp.bfloat16), (value - high).astype(jnp.bfloat16)

    cut = 64
    gathered = [(0, 32), (32, 32)]
    partial = [(64, 32), (96, 24)]

    perm = jnp.concatenate([kl_fields, mean_perm[None]], 0).reshape(terms, rows, nz)
    perm_down = widened(lax.ppermute(perm, "space", forward))
    perm_up = widened(lax.ppermute(perm, "space", backward))
    perm = widened(perm)

    received, bounds, low_row = [], [], 0
    for first, count in gathered:
        high_row = min(first + count + 1, rows)
        piece = own3[:, low_row:high_row].reshape(mode_dev * (high_row - low_row), nz)
        received.append([rotated(piece, s) for s in range(1, groups)])
        bounds.append((low_row, high_row - low_row))
        low_row = high_row
    halos = []
    for first, count in partial:
        piece = own3[:, first : first + count]
        halos.append((lax.ppermute(piece, "space", backward), lax.ppermute(piece, "space", forward)))

    high, low = split(jnp.concatenate([block(group, group - s) for s in range(groups)], 2))
    gathered_weights = jnp.concatenate([high, high, low], 2).reshape((terms - 1) * pad, 3 * groups * pad)
    high, low = split(jnp.concatenate([block(group + s, group) for s in range(groups)], 1))
    partial_weights = (
        jnp.concatenate([high, low], 1).transpose(1, 0, 2).reshape(2 * groups * pad, (terms - 1) * pad)
    )

    params = pltpu.CompilerParams(vmem_limit_bytes=LIMIT)
    f32 = jnp.float32
    result = None
    shape = (mode_dev, rows, nz)

    shares = []
    for (first, count), (up, down) in zip(partial, halos):
        flat = jax.ShapeDtypeStruct((mode_dev * count, nz), f32)
        outs = pl.pallas_call(
            functools.partial(partial_kernel, first, count, rows, mode_dev, pad, groups),
            in_specs=[VMEM] * 7,
            out_specs=[VMEM] * groups,
            out_shape=[flat] * groups,
            scratch_shapes=[
                pltpu.VMEM((FACES * terms, count, nz), f32),
                pltpu.VMEM((6, pad, nz), f32),
                pltpu.VMEM(((terms - 1) * pad, 2 * nz), jnp.bfloat16),
                pltpu.VMEM(((terms - 1) * pad, 2 * nz), jnp.bfloat16),
            ],
            compiler_params=params,
            name="partial",
        )(own, up.reshape(mode_dev * count, nz), down.reshape(mode_dev * count, nz), perm, perm_up, perm_down, partial_weights)
        parts = [outs[0]] + [rotated(value, s) for s, value in enumerate(outs[1:], 1)]
        shares.append((first, [part.reshape(mode_dev, count, nz) for part in parts]))

    for index, (first, count) in enumerate(gathered):
        begin = max(index - 1, 0)
        sources = bounds[begin : index + 1]
        pieces = [piece for group_pieces in received[begin : index + 1] for piece in group_pieces]
        flat = jax.ShapeDtypeStruct((mode_dev * count, nz), f32)
        centre, to_up, to_down = pl.pallas_call(
            functools.partial(
                gathered_kernel, first, count, rows, mode_dev, pad, groups, sources
            ),
            in_specs=[VMEM] * (5 + len(pieces)),
            out_specs=[VMEM] * 3,
            out_shape=[flat] * 3,
            scratch_shapes=[
                pltpu.VMEM((FACES * terms, count + SUB, nz), f32),
                pltpu.VMEM((2, groups, pad, nz), f32),
                pltpu.VMEM((3 * groups * pad, 2 * nz), jnp.bfloat16),
                pltpu.VMEM(((terms - 1) * pad, 2 * nz), f32),
                pltpu.VMEM((pad, nz), f32),
                pltpu.VMEM((pad, nz), f32),
            ],
            compiler_params=params,
            name="gathered",
        )(own, perm, perm_up, perm_down, gathered_weights, *pieces)
        parts = [centre, lax.ppermute(to_up, "space", forward), lax.ppermute(to_down, "space", backward)]
        shares.append((first, [part.reshape(mode_dev, count, nz) for part in parts]))

    for first, parts in shares:
        result = place_sum(result, parts, first, shape)
    return result.reshape(mode_coeffs.shape)


def solution(mesh):
    in_specs = (
        P("modes", "space", None, None),
        P("space", None, None),
        P(None, "space", None, None),
        P(),
    )
    out_specs = P("modes", "space", None, None)
    return jax.shard_map(local, mesh=mesh, in_specs=in_specs, out_specs=out_specs, check_vma=False)
```

```python
import functools
import math

import jax
import jax.numpy as jnp
from jax import lax
from jax.experimental import pallas as pl
from jax.experimental.pallas import tpu as pltpu
from jax.sharding import PartitionSpec as P

SUB = 8
PACK = 16
FACES = 6
LIMIT = 48 * 2**20
VMEM = pl.BlockSpec(memory_space=pltpu.VMEM)
ANY = pl.BlockSpec(memory_space=pl.ANY)


def halves(value):
    high = value.astype(jnp.bfloat16)
    low = (value - high.astype(jnp.float32)).astype(jnp.bfloat16)
    return high, low


def window_of(low_row, last, rows):
    base = low_row // SUB * SUB - SUB
    return base, (last // SUB + 2) * SUB - base


def fetch(copies, semaphores):
    started = []
    for index, (source, target) in enumerate(copies):
        started.append(pltpu.make_async_copy(source, target, semaphores.at[index]))
    for copy in started:
        copy.start()
    for copy in started:
        copy.wait()


def fetch_rows(own, perms, fields, near, base, size, rows, semaphores, more=()):
    begin, end = max(base, 0), min(base + size, rows)
    inside, there = pl.ds(begin, end - begin), pl.ds(begin - base, end - begin)
    terms = fields.shape[1]
    for edge, cells in ((0, begin - base), (end - base, base + size - end)):
        if cells:
            fields[0, :, pl.ds(edge, cells), :] = jnp.zeros((terms, cells, fields.shape[3]), fields.dtype)
    copies = [(own.at[:, inside, :], near.at[:, there, :])]
    for n, ref in enumerate(perms):
        copies.append((ref.at[:, inside, :], fields.at[n, :, there, :]))
    fetch(copies + list(more), semaphores)


def face_coefs(coef, fields, begin, count):
    terms, nz = fields.shape[1], fields.shape[3]
    span = coef.shape[0] // (FACES * terms)
    lane = lax.broadcasted_iota(jnp.int32, (count, nz), 1)
    for k in range(terms):
        here = fields[0, k, pl.ds(begin, count), :]
        others = (
            fields[1, k, pl.ds(begin, count), :],
            fields[2, k, pl.ds(begin, count), :],
            fields[0, k, pl.ds(begin + 1, count), :],
            fields[0, k, pl.ds(begin - 1, count), :],
            jnp.where(lane < nz - 1, pltpu.roll(here, nz - 1, 1), 0.0),
            jnp.where(lane > 0, pltpu.roll(here, 1, 1), 0.0),
        )
        for f, other in enumerate(others):
            coef[pl.ds((f * terms + k) * span, count), :] = 0.5 * (here + other)


def strided_rows(ref, start, count, stride):
    return ref[pl.ds(start, count, stride=stride), :]


def mode_block(ref, block, row, modes, stride):
    size = min(PACK, modes - block * PACK)
    value = strided_rows(ref, block * PACK * stride + row, size, stride)
    if size == PACK:
        return value
    return jnp.concatenate([value, jnp.zeros((PACK - size, value.shape[1]), value.dtype)], 0)


def factor_of(coef, at, terms, span):
    def factor(f, k):
        value = coef[pl.ds((f * terms + k) * span + at, SUB, stride=0), :]
        return jnp.concatenate([value] * (PACK // SUB), 0)

    return factor


def gathered_kernel(first, count, rows, mode_dev, pad, groups, sources, *refs):
    own_all, perm, perm_up, perm_down, weights = refs[:5]
    pieces = refs[5 : 5 + len(sources) * (groups - 1)]
    out, to_up, to_down = refs[5 + len(pieces) : 8 + len(pieces)]
    (
        near, fields, semaphores, coef, stack_even, stack_odd, mixed_even, mixed_odd, pending, above, beyond
    ) = refs[8 + len(pieces) :]
    terms, nz = fields.shape[1], fields.shape[3]
    low_row, last = max(first - 1, 0), min(first + count, rows - 1)
    span = coef.shape[0] // (FACES * terms)
    base, size = window_of(low_row, last, rows)
    perms = (perm, perm_up, perm_down)
    fetch_rows(own_all, perms, fields, near, base, size, rows, semaphores)
    own = near.reshape(mode_dev * size, nz)
    face_coefs(coef, fields, low_row - base, last - low_row + 1)
    lane = lax.broadcasted_iota(jnp.int32, (PACK, nz), 1)
    wide = groups * pad
    blocks = [(block, min(PACK, mode_dev - block * PACK)) for block in range(pad // PACK)]

    def fill(stack, slot, row, source):
        lanes = pl.ds(slot * nz, nz)
        start, length, index = source
        for s in range(groups):
            piece, at, stride = (own, row - base, size) if s == 0 else (pieces[index * (groups - 1) + s - 1], row - start, length)
            for block in range(pad // PACK):
                high, low = halves(mode_block(piece, block, at, mode_dev, stride))
                place = s * pad + block * PACK
                stack[place : place + PACK, lanes] = high
                stack[wide + place : wide + place + PACK, lanes] = low
                stack[2 * wide + place : 2 * wide + place + PACK, lanes] = high

    def mix(stack, mixed):
        mixed[...] = jnp.dot(weights[...], stack[...], preferred_element_type=jnp.float32)

    def sums(mixed, slot, row, block, faces):
        factor = factor_of(coef, row - low_row, terms, span)
        totals = [None] * len(faces)
        for k in range(terms):
            if k == terms - 1:
                value = mode_block(own, block, row - base, mode_dev, size)
            else:
                value = mixed[pl.ds(k * pad + block * PACK, PACK), pl.ds(slot * nz, nz)]
            for n, f in enumerate(faces):
                part = factor(f, k) * value
                totals[n] = part if totals[n] is None else totals[n] + part
        return totals

    def spread(mixed, row):
        for block, modes in blocks:
            here = pl.ds(block * PACK, PACK)
            here_out = block * PACK * count + row - first
            for slot in range(2):
                up, down, north, south, east, west = sums(mixed, slot, row + slot, block, range(FACES))
                place = pl.ds(here_out + slot, modes, stride=count)
                to_up[place, :] = -up[:modes]
                to_down[place, :] = -down[:modes]
                moved_east = jnp.where(lane > 0, pltpu.roll(east, 1, 1), 0.0)
                moved_west = jnp.where(lane < nz - 1, pltpu.roll(west, nz - 1, 1), 0.0)
                total = ((up + down) + (north + south)) + ((east - moved_east) + (west - moved_west))
                if slot == 0:
                    before = pending[here, :] - south
                    back = pl.ds(block * PACK * count + jnp.maximum(row - 1 - first, 0), modes, stride=count)
                    out[back, :] = before[:modes]
                    carried = total - above[here, :], north
                else:
                    out[pl.ds(here_out, modes, stride=count), :] = (carried[0] - south)[:modes]
                    pending[here, :] = total - carried[1]
                    above[here, :] = north

    def source_of(row):
        for index, (start, length) in reversed(list(enumerate(sources))):
            if row >= start:
                return start, length, index

    fill(stack_odd, 0, low_row, source_of(low_row))
    fill(stack_odd, 1, last, source_of(last))
    mix(stack_odd, mixed_odd)
    main = source_of(first)
    if main[2] != len(sources) - 1:
        late = source_of(last)
        fill(stack_even, 0, first, main)
        fill(stack_even, 1, first + 1, late)
        main = late
    else:
        fill(stack_even, 0, first, main)
        fill(stack_even, 1, first + 1, main)
    mix(stack_even, mixed_even)
    for block, modes in blocks:
        here = pl.ds(block * PACK, PACK)
        zero = jnp.zeros((PACK, nz), jnp.float32)
        above[here, :] = sums(mixed_odd, 0, low_row, block, [2])[0] if low_row < first else zero
        beyond[here, :] = sums(mixed_odd, 1, last, block, [3])[0] if last >= first + count else zero
        pending[here, :] = zero

    def body(step, carry):
        row = first + 4 * step
        fill(stack_odd, 0, row + 2, main)
        fill(stack_odd, 1, row + 3, main)
        mix(stack_odd, mixed_odd)
        spread(mixed_even, row)
        later = jnp.minimum(row + 4, first + count - 2)
        fill(stack_even, 0, later, main)
        fill(stack_even, 1, later + 1, main)
        mix(stack_even, mixed_even)
        spread(mixed_odd, row + 2)
        return carry

    lax.fori_loop(0, count // 4, body, 0)
    for block, modes in blocks:
        here = pl.ds(block * PACK, PACK)
        value = pending[here, :] - beyond[here, :]
        out[pl.ds(block * PACK * count + count - 1, modes, stride=count), :] = value[:modes]


def partial_kernel(first, count, rows, mode_dev, pad, groups, halo_first, *refs):
    own_all, up_all, down_all, perm, perm_up, perm_down, weights, out = refs[:8]
    sends = refs[8 : 8 + groups - 1]
    near, halo, fields, semaphores, coef, high_even, low_even, mean_even, high_odd, low_odd, mean_odd = refs[
        8 + groups - 1 :
    ]
    even, odd = (high_even, low_even, mean_even), (high_odd, low_odd, mean_odd)
    terms, nz = fields.shape[1], fields.shape[3]
    base, size = window_of(first, first + count - 1, rows)
    perms = (perm, perm_up, perm_down)
    here = pl.ds(first - halo_first, count)
    halos = [(up_all.at[:, here, :], halo.at[0]), (down_all.at[:, here, :], halo.at[1])]
    fetch_rows(own_all, perms, fields, near, base, size, rows, semaphores, halos)
    own = near.reshape(mode_dev * size, nz)
    up, down = halo.at[0].reshape(mode_dev * count, nz), halo.at[1].reshape(mode_dev * count, nz)
    face_coefs(coef, fields, first - base, count)
    lane = lax.broadcasted_iota(jnp.int32, (PACK, nz), 1)
    wide = groups * pad

    def build(store, row):
        high, low, mean = store
        for slot in range(2):
            lanes = pl.ds(slot * nz, nz)
            at = row + slot
            factor = factor_of(coef, at - first, terms, count)
            north_in, south_in = at + 1 < rows, at > 0
            for block in range(pad // PACK):
                centre = mode_block(own, block, at - base, mode_dev, size)
                north = mode_block(own, block, jnp.minimum(at + 1, rows - 1) - base, mode_dev, size)
                south = mode_block(own, block, jnp.maximum(at - 1, 0) - base, mode_dev, size)
                others = (
                    mode_block(up, block, at - first, mode_dev, count),
                    mode_block(down, block, at - first, mode_dev, count),
                    jnp.where(north_in, north, 0.0) if first + count == rows else north,
                    jnp.where(south_in, south, 0.0) if first == 0 else south,
                    jnp.where(lane < nz - 1, pltpu.roll(centre, nz - 1, 1), 0.0),
                    jnp.where(lane > 0, pltpu.roll(centre, 1, 1), 0.0),
                )
                steps = [centre - other for other in others]
                for k in range(terms):
                    total = factor(0, k) * steps[0]
                    for f in range(1, FACES):
                        total = total + factor(f, k) * steps[f]
                    if k == terms - 1:
                        mean[slot, pl.ds(block * PACK, PACK), :] = total
                    else:
                        place = pl.ds(k * pad + block * PACK, PACK)
                        high[place, lanes], low[place, lanes] = halves(total)

    def multiply(store, row):
        high, low, mean = store
        both = jnp.dot(weights[...], high[...], preferred_element_type=jnp.float32)
        rest = jnp.dot(weights[0:wide, :], low[...], preferred_element_type=jnp.float32)
        result = both[0:wide] + both[wide : 2 * wide] + rest
        for slot in range(2):
            lanes = slice(slot * nz, (slot + 1) * nz)
            for s in range(groups):
                target = out if s == 0 else sends[s - 1]
                value = result[s * pad : (s + 1) * pad, lanes]
                if s == 0:
                    value = value + mean[slot]
                target[pl.ds(row + slot - first, mode_dev, stride=count), :] = value[:mode_dev]

    build(even, first)

    def body(step, carry):
        row = first + 4 * step
        multiply(even, row)
        build(odd, row + 2)
        multiply(odd, row + 2)
        build(even, jnp.minimum(row + 4, first + count - 2))
        return carry

    lax.fori_loop(0, count // 4, body, 0)


def place_sum(result, parts, first, shape):
    modes, count, nz = parts[0].shape
    kept = [] if result is None else [result]
    steps = next(n for n in (2, 3, 1) if modes % n == 0)

    def kernel(*refs):
        *sources, out = refs[len(kept) :]
        total = sources[0][...]
        for source in sources[1:]:
            total = total + source[...]
        out[...] = total

    size = math.gcd(first, count)
    if size < count:
        steps = 1
    return pl.pallas_call(
        kernel,
        grid=(steps, count // size),
        in_specs=[pl.BlockSpec(memory_space=pl.ANY)] * len(kept)
        + [pl.BlockSpec((modes // steps, size, nz), lambda i, j: (i, j, 0))] * len(parts),
        out_specs=pl.BlockSpec((modes // steps, size, nz), lambda i, j: (i, j + first // size, 0)),
        out_shape=jax.ShapeDtypeStruct(shape, jnp.float32),
        input_output_aliases={0: 0} if kept else {},
        name="place",
    )(*kept, *parts)


def local(mode_coeffs, mean_perm, kl_fields, couplings):
    mode_dev, _, rows, nz = mode_coeffs.shape
    terms = kl_fields.shape[0] + 1
    groups = lax.axis_size("modes")
    planes = lax.axis_size("space")
    pad = pl.cdiv(mode_dev, PACK) * PACK
    group = lax.axis_index("modes")
    forward = [(i, i + 1) for i in range(planes - 1)]
    backward = [(target, source) for source, target in forward]
    own3 = mode_coeffs.reshape(mode_dev, rows, nz)

    def rotated(value, step):
        return lax.ppermute(value, "modes", [(i, (i + step) % groups) for i in range(groups)])

    def block(row_group, column_group):
        piece = lax.dynamic_slice(
            couplings,
            (0, (row_group % groups) * mode_dev, (column_group % groups) * mode_dev),
            (terms - 1, mode_dev, mode_dev),
        )
        return jnp.pad(piece, ((0, 0), (0, pad - mode_dev), (0, pad - mode_dev)))

    def split(value):
        high = lax.reduce_precision(value, 8, 7)
        return high.astype(jnp.bfloat16), (value - high).astype(jnp.bfloat16)

    gathered = [(0, 32), (32, 40)]
    partial = [(72, 24), (96, 24)]

    perm = jnp.concatenate([kl_fields, mean_perm[None]], 0).reshape(terms, rows, nz)
    perm_up, perm_down = lax.ppermute(perm, "space", backward), lax.ppermute(perm, "space", forward)
    received, bounds, low_row = [], [], 0
    for index, (first, count) in enumerate(gathered):
        high_row = min(first + count + 1, rows)
        piece = own3[:, low_row:high_row].reshape(mode_dev * (high_row - low_row), nz)
        if index:
            piece, perm_up, perm_down = lax.optimization_barrier((piece, perm_up, perm_down))
        received.append([rotated(piece, s) for s in range(1, groups)])
        bounds.append((low_row, high_row - low_row))
        low_row = high_row
    halo_first = partial[0][0]
    edge = own3[:, halo_first:]
    halos = lax.ppermute(edge, "space", backward), lax.ppermute(edge, "space", forward)

    high, low = split(jnp.concatenate([block(group, group - s) for s in range(groups)], 2))
    gathered_weights = jnp.concatenate([high, high, low], 2).reshape((terms - 1) * pad, 3 * groups * pad)
    high, low = split(jnp.concatenate([block(group + s, group) for s in range(groups)], 1))
    partial_weights = (
        jnp.concatenate([high, low], 1).transpose(1, 0, 2).reshape(2 * groups * pad, (terms - 1) * pad)
    )

    params = pltpu.CompilerParams(vmem_limit_bytes=LIMIT)
    f32 = jnp.float32
    result = None
    shape = (mode_dev, rows, nz)

    shares = []

    def window_scratch(first, count, around):
        _, size = window_of(max(first - around, 0), min(first + count - 1 + around, rows - 1), rows)
        return [
            pltpu.VMEM((mode_dev, size, nz), f32),
            pltpu.VMEM((3, terms, size, nz), f32),
            pltpu.SemaphoreType.DMA((6,)),
            pltpu.VMEM((FACES * terms * (count + around * SUB), nz), f32),
        ]

    def cost(count):
        products = 3 * 2 * (terms - 1) * mode_dev * mode_dev * groups * count * nz
        return pl.CostEstimate(flops=16 * products, bytes_accessed=2**20 * count, transcendentals=0)

    def partial_shares(index):
        first, count = partial[index]
        flat = jax.ShapeDtypeStruct((mode_dev * count, nz), f32)
        near, *rest = window_scratch(first, count, 0)
        outs = pl.pallas_call(
            functools.partial(partial_kernel, first, count, rows, mode_dev, pad, groups, halo_first),
            in_specs=[ANY] * 6 + [VMEM],
            out_specs=[VMEM] * groups,
            out_shape=[flat] * groups,
            scratch_shapes=[near, pltpu.VMEM((2, mode_dev, count, nz), f32), *rest]
            + [
                pltpu.VMEM(((terms - 1) * pad, 2 * nz), jnp.bfloat16),
                pltpu.VMEM(((terms - 1) * pad, 2 * nz), jnp.bfloat16),
                pltpu.VMEM((2, pad, nz), f32),
            ]
            * 2,
            compiler_params=params,
            cost_estimate=cost(count),
            name="partial",
        )(own3, *halos, perm, perm_up, perm_down, partial_weights)
        parts = [outs[0]] + [rotated(value, s) for s, value in enumerate(outs[1:], 1)]
        return first, [part.reshape(mode_dev, count, nz) for part in parts]

    def gathered_shares(index):
        first, count = gathered[index]
        begin = max(index - 1, 0)
        sources = bounds[begin : index + 1]
        pieces = [piece for group_pieces in received[begin : index + 1] for piece in group_pieces]
        flat = jax.ShapeDtypeStruct((mode_dev * count, nz), f32)
        centre, to_up, to_down = pl.pallas_call(
            functools.partial(
                gathered_kernel, first, count, rows, mode_dev, pad, groups, sources
            ),
            in_specs=[ANY] * 4 + [VMEM] * (1 + len(pieces)),
            out_specs=[VMEM] * 3,
            out_shape=[flat] * 3,
            scratch_shapes=window_scratch(first, count, 1)
            + [
                pltpu.VMEM((3 * groups * pad, 2 * nz), jnp.bfloat16),
                pltpu.VMEM((3 * groups * pad, 2 * nz), jnp.bfloat16),
                pltpu.VMEM(((terms - 1) * pad, 2 * nz), f32),
                pltpu.VMEM(((terms - 1) * pad, 2 * nz), f32),
                pltpu.VMEM((pad, nz), f32),
                pltpu.VMEM((pad, nz), f32),
                pltpu.VMEM((pad, nz), f32),
            ],
            compiler_params=params,
            cost_estimate=cost(count),
            name="gathered",
        )(own3, perm, perm_up, perm_down, gathered_weights, *pieces)
        parts = [centre, lax.ppermute(to_up, "space", forward), lax.ppermute(to_down, "space", backward)]
        return first, [part.reshape(mode_dev, count, nz) for part in parts]

    shares = [gathered_shares(0), partial_shares(0), partial_shares(1), gathered_shares(1)]
    for first, parts in shares:
        result = place_sum(result, parts, first, shape)
    return result.reshape(mode_coeffs.shape)


def solution(mesh):
    in_specs = (
        P("modes", "space", None, None),
        P("space", None, None),
        P(None, "space", None, None),
        P(),
    )
    out_specs = P("modes", "space", None, None)
    return jax.shard_map(local, mesh=mesh, in_specs=in_specs, out_specs=out_specs, check_vma=False)
```

```python
import functools

import jax
import jax.numpy as jnp
from jax import lax
from jax.experimental import pallas as pl
from jax.experimental.pallas import tpu as pltpu
from jax.sharding import PartitionSpec as P

SUB = 8
PACK = 16
FACES = 6
LIMIT = 48 * 2**20
VMEM = pl.BlockSpec(memory_space=pltpu.VMEM)
ANY = pl.BlockSpec(memory_space=pl.ANY)
HBM = pl.BlockSpec(memory_space=pltpu.HBM)


def halves(value):
    high = value.astype(jnp.bfloat16)
    low = (value - high.astype(jnp.float32)).astype(jnp.bfloat16)
    return high, low


def spaced(count):
    return count + SUB if count // SUB % 2 == 0 else count


def tile_copy(source, row, target, at, semaphore):
    return pltpu.make_async_copy(
        source.at[:, pl.ds(pl.multiple_of(row, SUB), SUB), :],
        target.at[:, pl.ds(pl.multiple_of(at, SUB), SUB), :],
        semaphore,
    )


def window_fields(perms, fields, first, count, rows, semaphores):
    begin, end = max(first - SUB, 0), min(first + count + SUB, rows)
    there = pl.ds(begin - first + SUB, end - begin)
    copies = []
    for n, ref in enumerate(perms):
        copies.append(
            pltpu.make_async_copy(ref.at[:, pl.ds(begin, end - begin), :], fields.at[n, :, there, :], semaphores.at[n])
        )
    for copy in copies:
        copy.start()
    return copies


def clear_outside(first, count, rows, fields, windows):
    for outside, at in ((first == 0, 0), (first + count == rows, count + SUB)):
        if outside:
            tile = pl.ds(at, SUB)
            fields[0, :, tile, :] = jnp.zeros((fields.shape[1], SUB, fields.shape[3]), fields.dtype)
            for ref in windows:
                ref[:, tile, :] = jnp.zeros((ref.shape[0], SUB, ref.shape[2]), ref.dtype)


def face_coefs(coef, fields, begin, count):
    terms, nz = fields.shape[1], fields.shape[3]
    span = coef.shape[0] // (FACES * terms)
    lane = lax.broadcasted_iota(jnp.int32, (count, nz), 1)
    for k in range(terms):
        here = fields[0, k, pl.ds(begin, count), :]
        others = (
            fields[1, k, pl.ds(begin, count), :],
            fields[2, k, pl.ds(begin, count), :],
            fields[0, k, pl.ds(begin + 1, count), :],
            fields[0, k, pl.ds(begin - 1, count), :],
            jnp.where(lane < nz - 1, pltpu.roll(here, nz - 1, 1), 0.0),
            jnp.where(lane > 0, pltpu.roll(here, 1, 1), 0.0),
        )
        for f, other in enumerate(others):
            coef[pl.ds((f * terms + k) * span, count), :] = 0.5 * (here + other)


def strided_rows(ref, start, count, stride):
    return ref[pl.ds(start, count, stride=stride), :]


def mode_block(ref, block, row, modes, stride):
    size = min(PACK, modes - block * PACK)
    value = strided_rows(ref, block * PACK * stride + row, size, stride)
    if size == PACK:
        return value
    return jnp.concatenate([value, jnp.zeros((PACK - size, value.shape[1]), value.dtype)], 0)


def factor_of(coef, at, terms, span):
    def factor(f, k):
        value = coef[pl.ds((f * terms + k) * span + at, SUB, stride=0), :]
        return jnp.concatenate([value] * (PACK // SUB), 0)

    return factor


def gathered_kernel(first, count, rows, mode_dev, pad, groups, sources, *refs):
    own_all, perm, perm_odd, perm_even, weights = refs[:5]
    pieces = refs[5 : 5 + len(sources) * (groups - 1)]
    results = refs[5 + len(pieces) : 8 + len(pieces)]
    near, far, fields, field_sems, in_sems, out_sems, coef = refs[8 + len(pieces) : 15 + len(pieces)]
    stack_even, mixed_even, stack_odd, mixed_odd, pending, above, *parts = refs[15 + len(pieces) :]
    terms, nz = fields.shape[1], fields.shape[3]
    span = coef.shape[0] // (FACES * terms)
    base, size = first - SUB, near.shape[1]
    tiles = count // SUB
    windows = [near] + [far.at[s] for s in range(groups - 1)]

    def tile_in(s, tile, index):
        row = base + tile * SUB
        if s == 0:
            return tile_copy(own_all, row, windows[0], tile * SUB, in_sems.at[0, tile])
        piece = pieces[index * (groups - 1) + s - 1]
        return tile_copy(piece, row - sources[index][0], windows[s], tile * SUB, in_sems.at[s, tile])

    def tile_out(n, tile):
        return tile_copy(parts[n], (tile + 1) * SUB, results[n], tile * SUB, out_sems.at[n, tile])

    field_copies = window_fields((perm, perm_odd, perm_even), fields, first, count, rows, field_sems)
    present = [tile for tile in range(tiles + 2) if 0 <= base + tile * SUB < rows]
    latest = len(sources) - 1
    early = {tile: max(latest - 1, 0) if tile < 2 else latest for tile in present}
    for tile in present:
        for s in range(groups):
            tile_in(s, tile, early[tile]).start()
    clear_outside(first, count, rows, fields, windows)
    for copy in field_copies:
        copy.wait()
    own, *others = [ref.reshape(mode_dev * size, nz) for ref in windows]
    tall = parts[0].shape[1]
    out, to_odd, to_even = [part.reshape(mode_dev * tall, nz) for part in parts]
    face_coefs(coef, fields, SUB - 1, span)
    pending[...] = jnp.zeros_like(pending)
    above[...] = jnp.zeros_like(above)
    lane = lax.broadcasted_iota(jnp.int32, (PACK, nz), 1)
    wide = groups * pad
    blocks = [(block, min(PACK, mode_dev - block * PACK)) for block in range(pad // PACK)]

    def mix(stack, mixed, row):
        for slot in range(2):
            lanes = pl.ds(slot * nz, nz)
            for s, piece in enumerate([own, *others]):
                for block, _ in blocks:
                    high, low = halves(mode_block(piece, block, row + slot - base, mode_dev, size))
                    place = s * pad + block * PACK
                    stack[place : place + PACK, lanes] = high
                    stack[wide + place : wide + place + PACK, lanes] = low
                    stack[2 * wide + place : 2 * wide + place + PACK, lanes] = high
        mixed[...] = jnp.dot(weights[...], stack[...], preferred_element_type=jnp.float32)

    def spread(mixed, row):
        for block, modes in blocks:
            here = pl.ds(block * PACK, PACK)
            for slot in range(2):
                factor = factor_of(coef, row + slot - first + 1, terms, span)
                totals = [None] * FACES
                for k in range(terms):
                    if k == terms - 1:
                        value = mode_block(own, block, row + slot - base, mode_dev, size)
                    else:
                        value = mixed[pl.ds(k * pad + block * PACK, PACK), pl.ds(slot * nz, nz)]
                    for f in range(FACES):
                        part = factor(f, k) * value
                        totals[f] = part if totals[f] is None else totals[f] + part
                odd, even, north, south, east, west = totals
                at = block * PACK * tall + row + slot - first + SUB
                place = pl.ds(at, modes, stride=tall)
                to_odd[place, :] = -odd[:modes]
                to_even[place, :] = -even[:modes]
                moved_east = jnp.where(lane > 0, pltpu.roll(east, 1, 1), 0.0)
                moved_west = jnp.where(lane < nz - 1, pltpu.roll(west, nz - 1, 1), 0.0)
                total = ((odd + even) + (north + south)) + ((east - moved_east) + (west - moved_west))
                back = pl.ds(at - 1, modes, stride=tall)
                if slot == 0:
                    out[back, :] = (pending[here, :] - south)[:modes]
                    carried = total - above[here, :], north
                else:
                    out[back, :] = (carried[0] - south)[:modes]
                    pending[here, :] = total - carried[1]
                    above[here, :] = north

    def wait_in(tile, index):
        for s in range(groups):
            tile_in(s, tile, index).wait()

    for tile in (0, 1):
        if tile in present:
            wait_in(tile, early[tile])
    mix(stack_even, mixed_even, first - 1)

    def four_rows(step, carry):
        row = first - 1 + 4 * step
        mix(stack_odd, mixed_odd, row + 2)
        spread(mixed_even, row)
        mix(stack_even, mixed_even, row + 4)
        spread(mixed_odd, row + 2)
        return carry

    def tile_step(tile, carry):
        @pl.when(tile < (tiles if tiles + 1 in present else tiles - 1))
        def _():
            wait_in(tile + 2, latest)

        lax.fori_loop(2 * tile, 2 * tile + 2, four_rows, 0)

        @pl.when(tile > 0)
        def _():
            for n in range(3):
                tile_out(n, tile - 1).start()

        return carry

    lax.fori_loop(0, tiles, tile_step, 0)
    spread(mixed_even, first - 1 + count)
    for n in range(3):
        tile_out(n, tiles - 1).start()
    for tile in range(tiles):
        for n in range(3):
            tile_out(n, tile).wait()


def partial_kernel(first, count, rows, mode_dev, pad, groups, halo_first, *refs):
    own_all, odd_all, even_all, perm, perm_odd, perm_even, weights = refs[:7]
    results = refs[7 : 7 + groups]
    near, halo, fields, field_sems, in_sems, out_sems, coef, high_even, low_even, mean_even, high_odd, low_odd, mean_odd, shares = refs[7 + groups :]
    even, odd = (high_even, low_even, mean_even), (high_odd, low_odd, mean_odd)
    terms, nz = fields.shape[1], fields.shape[3]
    base, size = first - SUB, near.shape[1]
    tall = halo.shape[2]
    tiles = count // SUB

    def near_in(tile):
        return tile_copy(own_all, base + tile * SUB, near, tile * SUB, in_sems.at[0, tile])

    def halo_in(side, tile):
        ref = (odd_all, even_all)[side]
        return tile_copy(ref, first - halo_first + tile * SUB, halo.at[side], tile * SUB, in_sems.at[1 + side, tile])

    def tile_out(s, tile):
        return tile_copy(shares.at[s], tile * SUB, results[s], tile * SUB, out_sems.at[s, tile])

    field_copies = window_fields((perm, perm_odd, perm_even), fields, first, count, rows, field_sems)
    present = [tile for tile in range(tiles + 2) if 0 <= base + tile * SUB < rows]
    for tile in range(tiles + 2):
        if tile in present:
            near_in(tile).start()
        if tile < tiles:
            halo_in(0, tile).start()
            halo_in(1, tile).start()
    clear_outside(first, count, rows, fields, [near])
    for copy in field_copies:
        copy.wait()
    own = near.reshape(mode_dev * size, nz)
    side_odd, side_even = halo.at[0].reshape(mode_dev * tall, nz), halo.at[1].reshape(mode_dev * tall, nz)
    parts = [shares.at[s].reshape(mode_dev * tall, nz) for s in range(groups)]
    face_coefs(coef, fields, SUB, count)
    lane = lax.broadcasted_iota(jnp.int32, (PACK, nz), 1)
    wide = groups * pad

    def build(store, row):
        high, low, mean = store
        for slot in range(2):
            lanes = pl.ds(slot * nz, nz)
            at = row + slot
            factor = factor_of(coef, at - first, terms, count)
            for block in range(pad // PACK):
                centre = mode_block(own, block, at - base, mode_dev, size)
                others = (
                    mode_block(side_odd, block, at - first, mode_dev, tall),
                    mode_block(side_even, block, at - first, mode_dev, tall),
                    mode_block(own, block, at + 1 - base, mode_dev, size),
                    mode_block(own, block, at - 1 - base, mode_dev, size),
                    jnp.where(lane < nz - 1, pltpu.roll(centre, nz - 1, 1), 0.0),
                    jnp.where(lane > 0, pltpu.roll(centre, 1, 1), 0.0),
                )
                steps = [centre - other for other in others]
                for k in range(terms):
                    total = factor(0, k) * steps[0]
                    for f in range(1, FACES):
                        total = total + factor(f, k) * steps[f]
                    if k == terms - 1:
                        mean[slot, pl.ds(block * PACK, PACK), :] = total
                    else:
                        place = pl.ds(k * pad + block * PACK, PACK)
                        high[place, lanes], low[place, lanes] = halves(total)

    def multiply(store, row):
        high, low, mean = store
        both = jnp.dot(weights[...], high[...], preferred_element_type=jnp.float32)
        rest = jnp.dot(weights[0:wide, :], low[...], preferred_element_type=jnp.float32)
        result = both[0:wide] + both[wide : 2 * wide] + rest
        for slot in range(2):
            lanes = slice(slot * nz, (slot + 1) * nz)
            for s, part in enumerate(parts):
                value = result[s * pad : (s + 1) * pad, lanes]
                if s == 0:
                    value = value + mean[slot]
                part[pl.ds(row + slot - first, mode_dev, stride=tall), :] = value[:mode_dev]

    for tile in (0, 1):
        if tile in present:
            near_in(tile).wait()
    halo_in(0, 0).wait()
    halo_in(1, 0).wait()
    build(even, first)

    def four_rows(step, carry):
        row = first + 4 * step
        multiply(even, row)
        build(odd, row + 2)
        multiply(odd, row + 2)
        build(even, jnp.minimum(row + 4, first + count - 2))
        return carry

    def tile_step(tile, carry):
        @pl.when(tile < (tiles if tiles + 1 in present else tiles - 1))
        def _():
            near_in(tile + 2).wait()

        @pl.when(tile + 1 < tiles)
        def _():
            halo_in(0, tile + 1).wait()
            halo_in(1, tile + 1).wait()

        lax.fori_loop(2 * tile, 2 * tile + 2, four_rows, 0)
        for s in range(groups):
            tile_out(s, tile).start()
        return carry

    lax.fori_loop(0, tiles, tile_step, 0)
    for tile in range(tiles):
        for s in range(groups):
            tile_out(s, tile).wait()


def place_sum(result, parts, first, shape):
    modes, count, nz = parts[0].shape
    kept = [] if result is None else [result]
    steps = next(n for n in (4, 3, 1) if modes % n == 0)
    some = modes // steps

    def kernel(*refs):
        sources = refs[len(kept) : len(kept) + len(parts)]
        out, near, total, in_sems, out_sems = refs[len(kept) + len(parts) :]
        copies_in = [
            [
                pltpu.make_async_copy(
                    source.at[pl.ds(step * some, some)], near.at[n, pl.ds(step * some, some)], in_sems.at[n, step]
                )
                for n, source in enumerate(sources)
            ]
            for step in range(steps)
        ]
        for copies in copies_in:
            for copy in copies:
                copy.start()
        copies_out = []
        for step, copies in enumerate(copies_in):
            here = pl.ds(step * some, some)
            for copy in copies:
                copy.wait()
            value = near[0, here]
            for n in range(1, len(parts)):
                value = value + near[n, here]
            total[here] = value
            copies_out.append(
                pltpu.make_async_copy(total.at[here], out.at[here, pl.ds(first, count), :], out_sems.at[step])
            )
            copies_out[-1].start()
        for copy in copies_out:
            copy.wait()

    return pl.pallas_call(
        kernel,
        in_specs=[ANY] * (len(kept) + len(parts)),
        out_specs=ANY,
        out_shape=jax.ShapeDtypeStruct(shape, jnp.float32),
        scratch_shapes=[
            pltpu.VMEM((len(parts), modes, count, nz), jnp.float32),
            pltpu.VMEM((modes, count, nz), jnp.float32),
            pltpu.SemaphoreType.DMA((len(parts), steps)),
            pltpu.SemaphoreType.DMA((steps,)),
        ],
        compiler_params=pltpu.CompilerParams(vmem_limit_bytes=LIMIT),
        input_output_aliases={0: 0} if kept else {},
        name="place",
    )(*kept, *parts)


def local(mode_coeffs, mean_perm, kl_fields, couplings):
    mode_dev, _, rows, nz = mode_coeffs.shape
    terms = kl_fields.shape[0] + 1
    groups = lax.axis_size("modes")
    planes = lax.axis_size("space")
    pad = pl.cdiv(mode_dev, PACK) * PACK
    group = lax.axis_index("modes")
    pairs = [
        [pair for i in range(start, planes - 1, 2) for pair in ((i, i + 1), (i + 1, i))] for start in (1, 0)
    ]
    own3 = mode_coeffs.reshape(mode_dev, rows, nz)

    def swapped(value, side):
        return lax.ppermute(value, "space", pairs[side])

    def rotated(value, step):
        return lax.ppermute(value, "modes", [(i, (i + step) % groups) for i in range(groups)])

    def block(row_group, column_group):
        piece = lax.dynamic_slice(
            couplings,
            (0, (row_group % groups) * mode_dev, (column_group % groups) * mode_dev),
            (terms - 1, mode_dev, mode_dev),
        )
        return jnp.pad(piece, ((0, 0), (0, pad - mode_dev), (0, pad - mode_dev)))

    def split(value):
        high = lax.reduce_precision(value, 8, 7)
        return high.astype(jnp.bfloat16), (value - high).astype(jnp.bfloat16)

    quarter = pl.cdiv(pl.cdiv(rows, 4), SUB) * SUB
    gathered = [(0, quarter), (quarter, quarter + SUB)]
    begin = 2 * quarter + SUB
    half = (rows - begin) // 2 // SUB * SUB
    partial = [(begin, half), (begin + half, rows - begin - half)]

    high, low = split(jnp.concatenate([block(group, group - s) for s in range(groups)], 2))
    gathered_weights = jnp.concatenate([high, high, low], 2).reshape((terms - 1) * pad, 3 * groups * pad)
    high, low = split(jnp.concatenate([block(group + s, group) for s in range(groups)], 1))
    partial_weights = (
        jnp.concatenate([high, low], 1).transpose(1, 0, 2).reshape(2 * groups * pad, (terms - 1) * pad)
    )

    perm = jnp.concatenate([kl_fields, mean_perm[None]], 0).reshape(terms, rows, nz)
    perm, ready = lax.optimization_barrier((perm, own3))
    bounds = [(0, gathered[1][0] + SUB), (gathered[1][0] + SUB, gathered[1][1])]
    piece, later_piece = [ready[:, start : start + length] for start, length in bounds]
    edge = ready[:, begin:]
    perm_odd, perm_even = swapped(perm, 0), swapped(perm, 1)
    arrived = [rotated(piece, s) for s in range(1, groups)]
    edge, perm_odd, perm_even, gathered_weights, partial_weights = lax.optimization_barrier(
        (edge, perm_odd, perm_even, gathered_weights, partial_weights)
    )
    halos = [swapped(edge, 0), swapped(edge, 1)]
    later_piece, arrived = lax.optimization_barrier((later_piece, arrived))
    received = [arrived, [rotated(later_piece, s) for s in range(1, groups)]]

    params = pltpu.CompilerParams(vmem_limit_bytes=LIMIT)
    f32 = jnp.float32
    result = None
    shape = (mode_dev, rows, nz)

    shares = []

    def window_scratch(count, around, inputs, outputs):
        size = count + 2 * SUB
        tiles = size // SUB
        return [
            pltpu.VMEM((3, terms, size, nz), f32),
            pltpu.SemaphoreType.DMA((3,)),
            pltpu.SemaphoreType.DMA((inputs, tiles)),
            pltpu.SemaphoreType.DMA((outputs, tiles)),
            pltpu.VMEM((FACES * terms * (count + around * SUB), nz), f32),
        ]

    def window_modes(count):
        return mode_dev, spaced(count + 2 * SUB), nz

    def cost(count):
        products = 3 * 2 * (terms - 1) * mode_dev * mode_dev * groups * count * nz
        return pl.CostEstimate(flops=products // 1024, bytes_accessed=2**10 * count, transcendentals=0)

    def partial_shares(index, source):
        first, count = partial[index]
        flat = jax.ShapeDtypeStruct((mode_dev, count, nz), f32)
        outs = pl.pallas_call(
            functools.partial(partial_kernel, first, count, rows, mode_dev, pad, groups, partial[0][0]),
            in_specs=[HBM] * 6 + [VMEM],
            out_specs=[HBM] * groups,
            out_shape=[flat] * groups,
            scratch_shapes=[pltpu.VMEM(window_modes(count), f32), pltpu.VMEM((2, mode_dev, spaced(count), nz), f32)]
            + window_scratch(count, 0, 3, groups)
            + [
                pltpu.VMEM(((terms - 1) * pad, 2 * nz), jnp.bfloat16),
                pltpu.VMEM(((terms - 1) * pad, 2 * nz), jnp.bfloat16),
                pltpu.VMEM((2, pad, nz), f32),
            ]
            * 2
            + [pltpu.VMEM((groups, mode_dev, spaced(count), nz), f32)],
            compiler_params=params,
            cost_estimate=cost(count),
            name="partial",
        )(source, *halos, perm, perm_odd, perm_even, partial_weights)
        parts = [outs[0]] + [rotated(value, s) for s, value in enumerate(outs[1:], 1)]
        return first, parts

    def gathered_shares(index, source):
        first, count = gathered[index]
        sources = bounds[: index + 1]
        pieces = [piece for group_pieces in received[: index + 1] for piece in group_pieces]
        flat = jax.ShapeDtypeStruct((mode_dev, count, nz), f32)
        centre, to_odd, to_even = pl.pallas_call(
            functools.partial(
                gathered_kernel, first, count, rows, mode_dev, pad, groups, sources
            ),
            in_specs=[HBM] * 4 + [VMEM] + [HBM] * len(pieces),
            out_specs=[HBM] * 3,
            out_shape=[flat] * 3,
            scratch_shapes=[pltpu.VMEM(window_modes(count), f32), pltpu.VMEM((groups - 1, *window_modes(count)), f32)]
            + window_scratch(count, 1, groups, 3)
            + [
                pltpu.VMEM((3 * groups * pad, 2 * nz), jnp.bfloat16),
                pltpu.VMEM(((terms - 1) * pad, 2 * nz), f32),
            ]
            * 2
            + [pltpu.VMEM((pad, nz), f32)] * 2
            + [pltpu.VMEM(window_modes(count), f32)] * 3,
            compiler_params=params,
            cost_estimate=cost(count),
            name="gathered",
        )(source, perm, perm_odd, perm_even, gathered_weights, *pieces)
        if index == 0:
            to_odd, to_even, *halos[:] = lax.optimization_barrier((to_odd, to_even, *halos))
        parts = [centre, swapped(to_odd, 0), swapped(to_even, 1)]
        return first, parts

    shares, source = [], own3
    for compute, index in ((gathered_shares, 0), (partial_shares, 0), (gathered_shares, 1), (partial_shares, 1)):
        if len(shares) == 3:
            source, shares[0][1][1:], shares[1][1][1:] = lax.optimization_barrier(
                (source, shares[0][1][1:], shares[1][1][1:])
            )
        share = compute(index, source)
        source, share[1][0] = lax.optimization_barrier((source, share[1][0]))
        shares.append(share)
    shares.append(shares.pop(2))
    for first, parts in shares:
        result = place_sum(result, parts, first, shape)
    return result.reshape(mode_coeffs.shape)


def solution(mesh):
    in_specs = (
        P("modes", "space", None, None),
        P("space", None, None),
        P(None, "space", None, None),
        P(),
    )
    out_specs = P("modes", "space", None, None)
    return jax.shard_map(local, mesh=mesh, in_specs=in_specs, out_specs=out_specs, check_vma=False)
```

```python
import functools

import jax
import jax.numpy as jnp
from jax import lax
from jax.experimental import pallas as pl
from jax.experimental.pallas import tpu as pltpu
from jax.sharding import PartitionSpec as P

SUB = 8
AHEAD = 3
PACK = 16
FACES = 6
LIMIT = 48 * 2**20
VMEM = pl.BlockSpec(memory_space=pltpu.VMEM)
ANY = pl.BlockSpec(memory_space=pl.ANY)
HBM = pl.BlockSpec(memory_space=pltpu.HBM)


def halves(value):
    high = value.astype(jnp.bfloat16)
    low = (value - high.astype(jnp.float32)).astype(jnp.bfloat16)
    return high, low


def spaced(count):
    return count + SUB if count // SUB % 2 == 0 else count


def tile_copy(source, row, target, at, semaphore):
    return pltpu.make_async_copy(
        source.at[:, pl.ds(pl.multiple_of(row, SUB), SUB), :],
        target.at[:, pl.ds(pl.multiple_of(at, SUB), SUB), :],
        semaphore,
    )


def window_fields(perms, fields, first, count, rows, semaphores):
    begin, end = max(first - SUB, 0), min(first + count + SUB, rows)
    there = pl.ds(begin - first + SUB, end - begin)
    copies = []
    for n, ref in enumerate(perms):
        copies.append(
            pltpu.make_async_copy(ref.at[:, pl.ds(begin, end - begin), :], fields.at[n, :, there, :], semaphores.at[n])
        )
    for copy in copies:
        copy.start()
    return copies


def clear_outside(first, count, rows, fields, windows):
    for outside, at in ((first == 0, 0), (first + count == rows, count + SUB)):
        if outside:
            tile = pl.ds(at, SUB)
            fields[0, :, tile, :] = jnp.zeros((fields.shape[1], SUB, fields.shape[3]), fields.dtype)
            for ref in windows:
                ref[:, tile, :] = jnp.zeros((ref.shape[0], SUB, ref.shape[2]), ref.dtype)


def face_coefs(coef, fields, begin, count):
    terms, nz = fields.shape[1], fields.shape[3]
    span = coef.shape[0] // (FACES * terms)
    lane = lax.broadcasted_iota(jnp.int32, (count, nz), 1)
    for k in range(terms):
        here = fields[0, k, pl.ds(begin, count), :]
        others = (
            fields[1, k, pl.ds(begin, count), :],
            fields[2, k, pl.ds(begin, count), :],
            fields[0, k, pl.ds(begin + 1, count), :],
            fields[0, k, pl.ds(begin - 1, count), :],
            jnp.where(lane < nz - 1, pltpu.roll(here, nz - 1, 1), 0.0),
            jnp.where(lane > 0, pltpu.roll(here, 1, 1), 0.0),
        )
        for f, other in enumerate(others):
            coef[pl.ds((f * terms + k) * span, count), :] = 0.5 * (here + other)


def strided_rows(ref, start, count, stride):
    return ref[pl.ds(start, count, stride=stride), :]


def mode_block(ref, block, row, modes, stride):
    size = min(PACK, modes - block * PACK)
    value = strided_rows(ref, block * PACK * stride + row, size, stride)
    if size == PACK:
        return value
    return jnp.concatenate([value, jnp.zeros((PACK - size, value.shape[1]), value.dtype)], 0)


def factor_of(coef, at, terms, span):
    def factor(f, k):
        value = coef[pl.ds((f * terms + k) * span + at, SUB, stride=0), :]
        return jnp.concatenate([value] * (PACK // SUB), 0)

    return factor


def gathered_kernel(first, count, rows, mode_dev, pad, groups, sources, *refs):
    own_all, perm, perm_odd, perm_even, weights = refs[:5]
    pieces = refs[5 : 5 + len(sources) * (groups - 1)]
    results = refs[5 + len(pieces) : 8 + len(pieces)]
    near, far, fields, field_sems, in_sems, out_sems, coef = refs[8 + len(pieces) : 15 + len(pieces)]
    stack_even, mixed_even, stack_odd, mixed_odd, pending, above, *parts = refs[15 + len(pieces) :]
    terms, nz = fields.shape[1], fields.shape[3]
    span = coef.shape[0] // (FACES * terms)
    base, size = first - SUB, near.shape[1]
    tiles = count // SUB
    windows = [near] + [far.at[s] for s in range(groups - 1)]

    def tile_in(s, tile, index):
        row = base + tile * SUB
        if s == 0:
            return tile_copy(own_all, row, windows[0], tile * SUB, in_sems.at[0, tile])
        piece = pieces[index * (groups - 1) + s - 1]
        return tile_copy(piece, row - sources[index][0], windows[s], tile * SUB, in_sems.at[s, tile])

    def tile_out(n, tile):
        return tile_copy(parts[n], (tile + 1) * SUB, results[n], tile * SUB, out_sems.at[n, tile])

    field_copies = window_fields((perm, perm_odd, perm_even), fields, first, count, rows, field_sems)
    present = [tile for tile in range(tiles + 2) if 0 <= base + tile * SUB < rows]
    latest = len(sources) - 1
    early = {tile: max(latest - 1, 0) if tile < 2 else latest for tile in present}
    def start_in(tile, index):
        for s in range(groups):
            tile_in(s, tile, index).start()

    for tile in present:
        if tile < AHEAD:
            start_in(tile, early[tile])
    clear_outside(first, count, rows, fields, windows)
    for copy in field_copies:
        copy.wait()
    own, *others = [ref.reshape(mode_dev * size, nz) for ref in windows]
    tall = parts[0].shape[1]
    out, to_odd, to_even = [part.reshape(mode_dev * tall, nz) for part in parts]
    face_coefs(coef, fields, SUB - 1, span)
    pending[...] = jnp.zeros_like(pending)
    above[...] = jnp.zeros_like(above)
    lane = lax.broadcasted_iota(jnp.int32, (PACK, nz), 1)
    wide = groups * pad
    blocks = [(block, min(PACK, mode_dev - block * PACK)) for block in range(pad // PACK)]

    def mix(stack, mixed, row):
        for slot in range(2):
            lanes = pl.ds(slot * nz, nz)
            for s, piece in enumerate([own, *others]):
                for block, _ in blocks:
                    high, low = halves(mode_block(piece, block, row + slot - base, mode_dev, size))
                    place = s * pad + block * PACK
                    stack[place : place + PACK, lanes] = high
                    stack[wide + place : wide + place + PACK, lanes] = low
                    stack[2 * wide + place : 2 * wide + place + PACK, lanes] = high
        mixed[...] = jnp.dot(weights[...], stack[...], preferred_element_type=jnp.float32)

    def spread(mixed, row):
        for block, modes in blocks:
            here = pl.ds(block * PACK, PACK)
            for slot in range(2):
                factor = factor_of(coef, row + slot - first + 1, terms, span)
                totals = [None] * FACES
                for k in range(terms):
                    if k == terms - 1:
                        value = mode_block(own, block, row + slot - base, mode_dev, size)
                    else:
                        value = mixed[pl.ds(k * pad + block * PACK, PACK), pl.ds(slot * nz, nz)]
                    for f in range(FACES):
                        part = factor(f, k) * value
                        totals[f] = part if totals[f] is None else totals[f] + part
                odd, even, north, south, east, west = totals
                at = block * PACK * tall + row + slot - first + SUB
                place = pl.ds(at, modes, stride=tall)
                to_odd[place, :] = -odd[:modes]
                to_even[place, :] = -even[:modes]
                moved_east = jnp.where(lane > 0, pltpu.roll(east, 1, 1), 0.0)
                moved_west = jnp.where(lane < nz - 1, pltpu.roll(west, nz - 1, 1), 0.0)
                total = ((odd + even) + (north + south)) + ((east - moved_east) + (west - moved_west))
                back = pl.ds(at - 1, modes, stride=tall)
                if slot == 0:
                    out[back, :] = (pending[here, :] - south)[:modes]
                    carried = total - above[here, :], north
                else:
                    out[back, :] = (carried[0] - south)[:modes]
                    pending[here, :] = total - carried[1]
                    above[here, :] = north

    def wait_in(tile, index):
        for s in range(groups):
            tile_in(s, tile, index).wait()

    for tile in (0, 1):
        if tile in present:
            wait_in(tile, early[tile])
    mix(stack_even, mixed_even, first - 1)

    def four_rows(step, carry):
        row = first - 1 + 4 * step
        mix(stack_odd, mixed_odd, row + 2)
        spread(mixed_even, row)
        mix(stack_even, mixed_even, row + 4)
        spread(mixed_odd, row + 2)
        return carry

    def tile_step(tile, carry):
        @pl.when(tile + AHEAD <= present[-1])
        def _():
            start_in(tile + AHEAD, latest)

        @pl.when(tile + 2 <= present[-1])
        def _():
            wait_in(tile + 2, latest)

        lax.fori_loop(2 * tile, 2 * tile + 2, four_rows, 0)

        @pl.when(tile > 0)
        def _():
            for n in range(3):
                tile_out(n, tile - 1).start()

        return carry

    lax.fori_loop(0, tiles, tile_step, 0)
    spread(mixed_even, first - 1 + count)
    for n in range(3):
        tile_out(n, tiles - 1).start()
    for tile in range(tiles):
        for n in range(3):
            tile_out(n, tile).wait()


def partial_kernel(first, count, rows, mode_dev, pad, groups, halo_first, *refs):
    own_all, odd_all, even_all, perm, perm_odd, perm_even, weights = refs[:7]
    results = refs[7 : 7 + groups]
    near, halo, fields, field_sems, in_sems, out_sems, coef, high_even, low_even, mean_even, high_odd, low_odd, mean_odd, shares, table = refs[7 + groups :]
    even, odd = (high_even, low_even, mean_even), (high_odd, low_odd, mean_odd)
    terms, nz = fields.shape[1], fields.shape[3]
    base, size = first - SUB, near.shape[1]
    tall = halo.shape[2]
    tiles = count // SUB

    def near_in(tile):
        return tile_copy(own_all, base + tile * SUB, near, tile * SUB, in_sems.at[0, tile])

    def halo_in(side, tile):
        ref = (odd_all, even_all)[side]
        return tile_copy(ref, first - halo_first + tile * SUB, halo.at[side], tile * SUB, in_sems.at[1 + side, tile])

    def tile_out(s, tile):
        return tile_copy(shares.at[s], tile * SUB, results[s], tile * SUB, out_sems.at[s, tile])

    field_copies = window_fields((perm, perm_odd, perm_even), fields, first, count, rows, field_sems)
    present = [tile for tile in range(tiles + 2) if 0 <= base + tile * SUB < rows]
    def start_halos(tile):
        halo_in(0, tile).start()
        halo_in(1, tile).start()

    for tile in range(AHEAD):
        if tile in present:
            near_in(tile).start()
        if tile < min(AHEAD - 1, tiles):
            start_halos(tile)
    clear_outside(first, count, rows, fields, [near])
    for k in range(weights.shape[0]):
        table[:, k * pad : (k + 1) * pad] = weights[k]
    for copy in field_copies:
        copy.wait()
    own = near.reshape(mode_dev * size, nz)
    side_odd, side_even = halo.at[0].reshape(mode_dev * tall, nz), halo.at[1].reshape(mode_dev * tall, nz)
    parts = [shares.at[s].reshape(mode_dev * tall, nz) for s in range(groups)]
    face_coefs(coef, fields, SUB, count)
    lane = lax.broadcasted_iota(jnp.int32, (PACK, nz), 1)
    wide = groups * pad

    def build(store, row):
        high, low, mean = store
        for slot in range(2):
            lanes = pl.ds(slot * nz, nz)
            at = row + slot
            factor = factor_of(coef, at - first, terms, count)
            for block in range(pad // PACK):
                centre = mode_block(own, block, at - base, mode_dev, size)
                others = (
                    mode_block(side_odd, block, at - first, mode_dev, tall),
                    mode_block(side_even, block, at - first, mode_dev, tall),
                    mode_block(own, block, at + 1 - base, mode_dev, size),
                    mode_block(own, block, at - 1 - base, mode_dev, size),
                    jnp.where(lane < nz - 1, pltpu.roll(centre, nz - 1, 1), 0.0),
                    jnp.where(lane > 0, pltpu.roll(centre, 1, 1), 0.0),
                )
                steps = [centre - other for other in others]
                for k in range(terms):
                    total = factor(0, k) * steps[0]
                    for f in range(1, FACES):
                        total = total + factor(f, k) * steps[f]
                    if k == terms - 1:
                        mean[slot, pl.ds(block * PACK, PACK), :] = total
                    else:
                        place = pl.ds(k * pad + block * PACK, PACK)
                        high[place, lanes], low[place, lanes] = halves(total)

    def multiply(store, row):
        high, low, mean = store
        both = jnp.dot(table[...], high[...], preferred_element_type=jnp.float32)
        rest = jnp.dot(table[0:wide, :], low[...], preferred_element_type=jnp.float32)
        result = both[0:wide] + both[wide : 2 * wide] + rest
        for slot in range(2):
            lanes = slice(slot * nz, (slot + 1) * nz)
            for s, part in enumerate(parts):
                value = result[s * pad : (s + 1) * pad, lanes]
                if s == 0:
                    value = value + mean[slot]
                part[pl.ds(row + slot - first, mode_dev, stride=tall), :] = value[:mode_dev]

    for tile in (0, 1):
        if tile in present:
            near_in(tile).wait()
    halo_in(0, 0).wait()
    halo_in(1, 0).wait()
    build(even, first)

    def four_rows(step, carry):
        row = first + 4 * step
        multiply(even, row)
        build(odd, row + 2)
        multiply(odd, row + 2)
        build(even, jnp.minimum(row + 4, first + count - 2))
        return carry

    def tile_step(tile, carry):
        @pl.when(tile + AHEAD <= present[-1])
        def _():
            near_in(tile + AHEAD).start()

        @pl.when(tile + AHEAD - 1 < tiles)
        def _():
            start_halos(tile + AHEAD - 1)

        @pl.when(tile + 2 <= present[-1])
        def _():
            near_in(tile + 2).wait()

        @pl.when(tile + 1 < tiles)
        def _():
            halo_in(0, tile + 1).wait()
            halo_in(1, tile + 1).wait()

        lax.fori_loop(2 * tile, 2 * tile + 2, four_rows, 0)
        for s in range(groups):
            tile_out(s, tile).start()
        return carry

    lax.fori_loop(0, tiles, tile_step, 0)
    for tile in range(tiles):
        for s in range(groups):
            tile_out(s, tile).wait()


def place_sums(result, shares, shape):
    modes, _, nz = shape
    kept = [] if result is None else [result]
    steps = next(n for n in (4, 3, 1) if modes % n == 0)
    some = modes // steps
    flat = [part for _, parts in shares for part in parts]

    def kernel(*refs):
        sources = refs[len(kept) : len(kept) + len(flat)]
        out, *scratch = refs[len(kept) + len(flat) :]
        in_sems, out_sems = scratch[-2:]
        jobs, copies_out = [], []
        for step in range(steps):
            here = pl.ds(step * some, some)
            n = 0
            for (first, parts), total in zip(shares, scratch[len(flat) :]):
                copies = [
                    pltpu.make_async_copy(sources[m].at[here], scratch[m].at[here], in_sems.at[m, step])
                    for m in range(n, n + len(parts))
                ]
                for copy in copies:
                    copy.start()
                jobs.append((step, here, first, parts[0].shape[1], n, copies, total))
                n += len(parts)
        for number, (step, here, first, count, n, copies, total) in enumerate(jobs):
            for copy in copies:
                copy.wait()
            value = scratch[n][here]
            for m in range(n + 1, n + len(copies)):
                value = value + scratch[m][here]
            total[here] = value
            copies_out.append(
                pltpu.make_async_copy(total.at[here], out.at[here, pl.ds(first, count), :], out_sems.at[number])
            )
            copies_out[-1].start()
        for copy in copies_out:
            copy.wait()

    return pl.pallas_call(
        kernel,
        in_specs=[ANY] * (len(kept) + len(flat)),
        out_specs=ANY,
        out_shape=jax.ShapeDtypeStruct(shape, jnp.float32),
        scratch_shapes=[pltpu.VMEM(part.shape, jnp.float32) for part in flat]
        + [pltpu.VMEM(parts[0].shape, jnp.float32) for _, parts in shares]
        + [pltpu.SemaphoreType.DMA((len(flat), steps)), pltpu.SemaphoreType.DMA((steps * len(shares),))],
        compiler_params=pltpu.CompilerParams(vmem_limit_bytes=LIMIT),
        input_output_aliases={0: 0} if kept else {},
        name="place",
    )(*kept, *flat)


def local(mode_coeffs, mean_perm, kl_fields, couplings):
    mode_dev, _, rows, nz = mode_coeffs.shape
    terms = kl_fields.shape[0] + 1
    groups = lax.axis_size("modes")
    planes = lax.axis_size("space")
    pad = pl.cdiv(mode_dev, PACK) * PACK
    group = lax.axis_index("modes")
    pairs = [
        [pair for i in range(start, planes - 1, 2) for pair in ((i, i + 1), (i + 1, i))] for start in (1, 0)
    ]
    own3 = mode_coeffs.reshape(mode_dev, rows, nz)

    def swapped(value, side):
        return lax.ppermute(value, "space", pairs[side])

    def rotated(value, step):
        return lax.ppermute(value, "modes", [(i, (i + step) % groups) for i in range(groups)])

    def block(row_group, column_group):
        piece = lax.dynamic_slice(
            couplings,
            (0, (row_group % groups) * mode_dev, (column_group % groups) * mode_dev),
            (terms - 1, mode_dev, mode_dev),
        )
        return jnp.pad(piece, ((0, 0), (0, pad - mode_dev), (0, pad - mode_dev)))

    def split(value):
        high = lax.reduce_precision(value, 8, 7)
        return high.astype(jnp.bfloat16), (value - high).astype(jnp.bfloat16)

    quarter = pl.cdiv(pl.cdiv(rows, 4), SUB) * SUB
    gathered = [(0, quarter), (quarter, quarter + SUB)]
    begin = 2 * quarter + SUB
    half = (rows - begin) // 2 // SUB * SUB
    partial = [(begin, half), (begin + half, rows - begin - half)]

    high, low = split(jnp.concatenate([block(group, group - s) for s in range(groups)], 2))
    gathered_weights = jnp.concatenate([high, high, low], 2).reshape((terms - 1) * pad, 3 * groups * pad)
    high, low = split(jnp.concatenate([block(group + s, group) for s in range(groups)], 1))
    partial_weights = jnp.concatenate([high, low], 1)

    perm = jnp.concatenate([kl_fields, mean_perm[None]], 0).reshape(terms, rows, nz)
    perm, ready = lax.optimization_barrier((perm, own3))
    bounds = [(0, gathered[1][0] + SUB), (gathered[1][0] + SUB, gathered[1][1])]
    piece, later_piece = [ready[:, start : start + length] for start, length in bounds]
    edge = ready[:, begin:]
    perm_odd, perm_even = swapped(perm, 0), swapped(perm, 1)
    arrived = [rotated(piece, s) for s in range(1, groups)]
    edge, perm_odd, perm_even, gathered_weights, partial_weights = lax.optimization_barrier(
        (edge, perm_odd, perm_even, gathered_weights, partial_weights)
    )
    halos = [swapped(edge, 0), swapped(edge, 1)]
    later_piece, arrived = lax.optimization_barrier((later_piece, arrived))
    received = [arrived, [rotated(later_piece, s) for s in range(1, groups)]]

    params = pltpu.CompilerParams(vmem_limit_bytes=LIMIT)
    f32 = jnp.float32
    shape = (mode_dev, rows, nz)

    shares = []

    def window_scratch(count, around, inputs, outputs):
        size = count + 2 * SUB
        tiles = size // SUB
        return [
            pltpu.VMEM((3, terms, size, nz), f32),
            pltpu.SemaphoreType.DMA((3,)),
            pltpu.SemaphoreType.DMA((inputs, tiles)),
            pltpu.SemaphoreType.DMA((outputs, tiles)),
            pltpu.VMEM((FACES * terms * (count + around * SUB), nz), f32),
        ]

    def window_modes(count):
        return mode_dev, spaced(count + 2 * SUB), nz

    def cost(count):
        products = 3 * 2 * (terms - 1) * mode_dev * mode_dev * groups * count * nz
        return pl.CostEstimate(flops=products // 1024, bytes_accessed=2**10 * count, transcendentals=0)

    def partial_shares(index, source):
        first, count = partial[index]
        flat = jax.ShapeDtypeStruct((mode_dev, count, nz), f32)
        outs = pl.pallas_call(
            functools.partial(partial_kernel, first, count, rows, mode_dev, pad, groups, partial[0][0]),
            in_specs=[HBM] * 6 + [VMEM],
            out_specs=[HBM] * groups,
            out_shape=[flat] * groups,
            scratch_shapes=[pltpu.VMEM(window_modes(count), f32), pltpu.VMEM((2, mode_dev, spaced(count), nz), f32)]
            + window_scratch(count, 0, 3, groups)
            + [
                pltpu.VMEM(((terms - 1) * pad, 2 * nz), jnp.bfloat16),
                pltpu.VMEM(((terms - 1) * pad, 2 * nz), jnp.bfloat16),
                pltpu.VMEM((2, pad, nz), f32),
            ]
            * 2
            + [
                pltpu.VMEM((groups, mode_dev, spaced(count), nz), f32),
                pltpu.VMEM((2 * groups * pad, (terms - 1) * pad), jnp.bfloat16),
            ],
            compiler_params=params,
            cost_estimate=cost(count),
            name="partial",
        )(source, *halos, perm, perm_odd, perm_even, partial_weights)
        parts = [outs[0]] + [rotated(value, s) for s, value in enumerate(outs[1:], 1)]
        return first, parts

    def gathered_shares(index, source):
        first, count = gathered[index]
        sources = bounds[: index + 1]
        pieces = [piece for group_pieces in received[: index + 1] for piece in group_pieces]
        flat = jax.ShapeDtypeStruct((mode_dev, count, nz), f32)
        centre, to_odd, to_even = pl.pallas_call(
            functools.partial(
                gathered_kernel, first, count, rows, mode_dev, pad, groups, sources
            ),
            in_specs=[HBM] * 4 + [VMEM] + [HBM] * len(pieces),
            out_specs=[HBM] * 3,
            out_shape=[flat] * 3,
            scratch_shapes=[pltpu.VMEM(window_modes(count), f32), pltpu.VMEM((groups - 1, *window_modes(count)), f32)]
            + window_scratch(count, 1, groups, 3)
            + [
                pltpu.VMEM((3 * groups * pad, 2 * nz), jnp.bfloat16),
                pltpu.VMEM(((terms - 1) * pad, 2 * nz), f32),
            ]
            * 2
            + [pltpu.VMEM((pad, nz), f32)] * 2
            + [pltpu.VMEM(window_modes(count), f32)] * 3,
            compiler_params=params,
            cost_estimate=cost(count),
            name="gathered",
        )(source, perm, perm_odd, perm_even, gathered_weights, *pieces)
        if index == 0:
            to_odd, to_even, *halos[:] = lax.optimization_barrier((to_odd, to_even, *halos))
        parts = [centre, swapped(to_odd, 0), swapped(to_even, 1)]
        return first, parts

    shares, source = [], own3
    for compute, index in ((gathered_shares, 0), (partial_shares, 0), (gathered_shares, 1), (partial_shares, 1)):
        if len(shares) == 3:
            source, shares[0][1][1:], shares[1][1][1:] = lax.optimization_barrier(
                (source, shares[0][1][1:], shares[1][1][1:])
            )
        share = compute(index, source)
        source, share[1][0] = lax.optimization_barrier((source, share[1][0]))
        shares.append(share)
    result = place_sums(None, shares[:2], shape)
    result = place_sums(result, shares[2:], shape)
    return result.reshape(mode_coeffs.shape)


def solution(mesh):
    in_specs = (
        P("modes", "space", None, None),
        P("space", None, None),
        P(None, "space", None, None),
        P(),
    )
    out_specs = P("modes", "space", None, None)
    return jax.shard_map(local, mesh=mesh, in_specs=in_specs, out_specs=out_specs, check_vma=False)
```

```python
import functools

import jax
import jax.numpy as jnp
from jax import lax
from jax.experimental import pallas as pl
from jax.experimental.pallas import tpu as pltpu
from jax.sharding import PartitionSpec as P

SUB = 8
AHEAD = 3
PACK = 16
FACES = 6
LIMIT = 48 * 2**20
VMEM = pl.BlockSpec(memory_space=pltpu.VMEM)
ANY = pl.BlockSpec(memory_space=pl.ANY)
HBM = pl.BlockSpec(memory_space=pltpu.HBM)


def halves(value):
    high = value.astype(jnp.bfloat16)
    low = (value - high.astype(jnp.float32)).astype(jnp.bfloat16)
    return high, low


def spaced(count):
    return count + SUB if count // SUB % 2 == 0 else count


def tile_copy(source, row, target, at, semaphore):
    return pltpu.make_async_copy(
        source.at[:, pl.ds(pl.multiple_of(row, SUB), SUB), :],
        target.at[:, pl.ds(pl.multiple_of(at, SUB), SUB), :],
        semaphore,
    )


def window_fields(perms, fields, first, count, rows, semaphores):
    begin, end = max(first - SUB, 0), min(first + count + SUB, rows)
    there = pl.ds(begin - first + SUB, end - begin)
    copies = []
    for n, ref in enumerate(perms):
        copies.append(
            pltpu.make_async_copy(ref.at[:, pl.ds(begin, end - begin), :], fields.at[n, :, there, :], semaphores.at[n])
        )
    for copy in copies:
        copy.start()
    return copies


def clear_outside(first, count, rows, fields, windows):
    for outside, at in ((first == 0, 0), (first + count == rows, count + SUB)):
        if outside:
            tile = pl.ds(at, SUB)
            fields[0, :, tile, :] = jnp.zeros((fields.shape[1], SUB, fields.shape[3]), fields.dtype)
            for ref in windows:
                ref[:, tile, :] = jnp.zeros((ref.shape[0], SUB, ref.shape[2]), ref.dtype)


def face_coefs(coef, fields, begin, count):
    terms, nz = fields.shape[1], fields.shape[3]
    span = coef.shape[0] // (FACES * terms)
    lane = lax.broadcasted_iota(jnp.int32, (count, nz), 1)
    for k in range(terms):
        here = fields[0, k, pl.ds(begin, count), :]
        others = (
            fields[1, k, pl.ds(begin, count), :],
            fields[2, k, pl.ds(begin, count), :],
            fields[0, k, pl.ds(begin + 1, count), :],
            fields[0, k, pl.ds(begin - 1, count), :],
            jnp.where(lane < nz - 1, pltpu.roll(here, nz - 1, 1), 0.0),
            jnp.where(lane > 0, pltpu.roll(here, 1, 1), 0.0),
        )
        for f, other in enumerate(others):
            coef[pl.ds((f * terms + k) * span, count), :] = 0.5 * (here + other)


def strided_rows(ref, start, count, stride):
    return ref[pl.ds(start, count, stride=stride), :]


def mode_block(ref, block, row, modes, stride):
    size = min(PACK, modes - block * PACK)
    value = strided_rows(ref, block * PACK * stride + row, size, stride)
    if size == PACK:
        return value
    return jnp.concatenate([value, jnp.zeros((PACK - size, value.shape[1]), value.dtype)], 0)


def factor_of(coef, at, terms, span):
    def factor(f, k):
        value = coef[pl.ds((f * terms + k) * span + at, SUB, stride=0), :]
        return jnp.concatenate([value] * (PACK // SUB), 0)

    return factor


def gathered_kernel(first, count, rows, mode_dev, pad, groups, sources, *refs):
    own_all, perm, perm_odd, perm_even, weights = refs[:5]
    pieces = refs[5 : 5 + len(sources) * (groups - 1)]
    results = refs[5 + len(pieces) : 8 + len(pieces)]
    near, far, fields, field_sems, in_sems, out_sems, coef = refs[8 + len(pieces) : 15 + len(pieces)]
    stack_even, mixed_even, stack_odd, mixed_odd, pending, above, *parts = refs[15 + len(pieces) :]
    terms, nz = fields.shape[1], fields.shape[3]
    span = coef.shape[0] // (FACES * terms)
    base, size = first - SUB, near.shape[1]
    tiles = count // SUB
    windows = [near] + [far.at[s] for s in range(groups - 1)]

    def tile_in(s, tile, index):
        row = base + tile * SUB
        if s == 0:
            return tile_copy(own_all, row, windows[0], tile * SUB, in_sems.at[0, tile])
        piece = pieces[index * (groups - 1) + s - 1]
        return tile_copy(piece, row - sources[index][0], windows[s], tile * SUB, in_sems.at[s, tile])

    def tile_out(n, tile):
        return tile_copy(parts[n], (tile + 1) * SUB, results[n], tile * SUB, out_sems.at[n, tile])

    field_copies = window_fields((perm, perm_odd, perm_even), fields, first, count, rows, field_sems)
    present = [tile for tile in range(tiles + 2) if 0 <= base + tile * SUB < rows]
    latest = len(sources) - 1
    early = {tile: max(latest - 1, 0) if tile < 2 else latest for tile in present}
    def start_in(tile, index):
        for s in range(groups):
            tile_in(s, tile, index).start()

    for tile in present:
        if tile < AHEAD:
            start_in(tile, early[tile])
    clear_outside(first, count, rows, fields, windows)
    for copy in field_copies:
        copy.wait()
    own, *others = [ref.reshape(mode_dev * size, nz) for ref in windows]
    tall = parts[0].shape[1]
    out, to_odd, to_even = [part.reshape(mode_dev * tall, nz) for part in parts]
    face_coefs(coef, fields, SUB - 1, span)
    pending[...] = jnp.zeros_like(pending)
    above[...] = jnp.zeros_like(above)
    lane = lax.broadcasted_iota(jnp.int32, (PACK, nz), 1)
    wide = groups * pad
    blocks = [(block, min(PACK, mode_dev - block * PACK)) for block in range(pad // PACK)]

    def mix(stack, mixed, row):
        for slot in range(2):
            lanes = pl.ds(slot * nz, nz)
            for s, piece in enumerate([own, *others]):
                for block, _ in blocks:
                    high, low = halves(mode_block(piece, block, row + slot - base, mode_dev, size))
                    place = s * pad + block * PACK
                    stack[place : place + PACK, lanes] = high
                    stack[wide + place : wide + place + PACK, lanes] = low
                    stack[2 * wide + place : 2 * wide + place + PACK, lanes] = high
        mixed[...] = jnp.dot(weights[...], stack[...], preferred_element_type=jnp.float32)

    def spread(mixed, row):
        for block, modes in blocks:
            here = pl.ds(block * PACK, PACK)
            for slot in range(2):
                factor = factor_of(coef, row + slot - first + 1, terms, span)
                totals = [None] * FACES
                for k in range(terms):
                    if k == terms - 1:
                        value = mode_block(own, block, row + slot - base, mode_dev, size)
                    else:
                        value = mixed[pl.ds(k * pad + block * PACK, PACK), pl.ds(slot * nz, nz)]
                    for f in range(FACES):
                        part = factor(f, k) * value
                        totals[f] = part if totals[f] is None else totals[f] + part
                odd, even, north, south, east, west = totals
                at = block * PACK * tall + row + slot - first + SUB
                place = pl.ds(at, modes, stride=tall)
                to_odd[place, :] = -odd[:modes]
                to_even[place, :] = -even[:modes]
                moved_east = jnp.where(lane > 0, pltpu.roll(east, 1, 1), 0.0)
                moved_west = jnp.where(lane < nz - 1, pltpu.roll(west, nz - 1, 1), 0.0)
                total = ((odd + even) + (north + south)) + ((east - moved_east) + (west - moved_west))
                back = pl.ds(at - 1, modes, stride=tall)
                if slot == 0:
                    out[back, :] = (pending[here, :] - south)[:modes]
                    carried = total - above[here, :], north
                else:
                    out[back, :] = (carried[0] - south)[:modes]
                    pending[here, :] = total - carried[1]
                    above[here, :] = north

    def wait_in(tile, index):
        for s in range(groups):
            tile_in(s, tile, index).wait()

    for tile in (0, 1):
        if tile in present:
            wait_in(tile, early[tile])
    mix(stack_even, mixed_even, first - 1)

    def four_rows(step, carry):
        row = first - 1 + 4 * step
        mix(stack_odd, mixed_odd, row + 2)
        spread(mixed_even, row)
        mix(stack_even, mixed_even, row + 4)
        spread(mixed_odd, row + 2)
        return carry

    def tile_step(tile, carry):
        @pl.when(tile + AHEAD <= present[-1])
        def _():
            start_in(tile + AHEAD, latest)

        @pl.when(tile + 2 <= present[-1])
        def _():
            wait_in(tile + 2, latest)

        lax.fori_loop(2 * tile, 2 * tile + 2, four_rows, 0)

        @pl.when(tile > 0)
        def _():
            for n in range(3):
                tile_out(n, tile - 1).start()

        return carry

    lax.fori_loop(0, tiles, tile_step, 0)
    spread(mixed_even, first - 1 + count)
    for n in range(3):
        tile_out(n, tiles - 1).start()
    for tile in range(tiles):
        for n in range(3):
            tile_out(n, tile).wait()


def partial_kernel(first, count, rows, mode_dev, pad, groups, halo_first, *refs):
    own_all, odd_all, even_all, perm, perm_odd, perm_even, weights = refs[:7]
    results = refs[7 : 7 + groups]
    near, halo, fields, field_sems, in_sems, out_sems, coef, high_even, low_even, mean_even, high_odd, low_odd, mean_odd, shares, table = refs[7 + groups :]
    even, odd = (high_even, low_even, mean_even), (high_odd, low_odd, mean_odd)
    terms, nz = fields.shape[1], fields.shape[3]
    base, size = first - SUB, near.shape[1]
    tall = halo.shape[2]
    tiles = count // SUB

    def near_in(tile):
        return tile_copy(own_all, base + tile * SUB, near, tile * SUB, in_sems.at[0, tile])

    def halo_in(side, tile):
        ref = (odd_all, even_all)[side]
        return tile_copy(ref, first - halo_first + tile * SUB, halo.at[side], tile * SUB, in_sems.at[1 + side, tile])

    def tile_out(s, tile):
        return tile_copy(shares.at[s], tile * SUB, results[s], tile * SUB, out_sems.at[s, tile])

    field_copies = window_fields((perm, perm_odd, perm_even), fields, first, count, rows, field_sems)
    present = [tile for tile in range(tiles + 2) if 0 <= base + tile * SUB < rows]
    def start_halos(tile):
        halo_in(0, tile).start()
        halo_in(1, tile).start()

    for tile in range(AHEAD):
        if tile in present:
            near_in(tile).start()
        if tile < min(AHEAD - 1, tiles):
            start_halos(tile)
    clear_outside(first, count, rows, fields, [near])
    for k in range(weights.shape[0]):
        table[:, k * pad : (k + 1) * pad] = weights[k]
    for copy in field_copies:
        copy.wait()
    own = near.reshape(mode_dev * size, nz)
    side_odd, side_even = halo.at[0].reshape(mode_dev * tall, nz), halo.at[1].reshape(mode_dev * tall, nz)
    parts = [shares.at[s].reshape(mode_dev * tall, nz) for s in range(groups)]
    face_coefs(coef, fields, SUB, count)
    lane = lax.broadcasted_iota(jnp.int32, (PACK, nz), 1)
    wide = groups * pad

    def build(store, row):
        high, low, mean = store
        for slot in range(2):
            lanes = pl.ds(slot * nz, nz)
            at = row + slot
            factor = factor_of(coef, at - first, terms, count)
            for block in range(pad // PACK):
                centre = mode_block(own, block, at - base, mode_dev, size)
                others = (
                    mode_block(side_odd, block, at - first, mode_dev, tall),
                    mode_block(side_even, block, at - first, mode_dev, tall),
                    mode_block(own, block, at + 1 - base, mode_dev, size),
                    mode_block(own, block, at - 1 - base, mode_dev, size),
                    jnp.where(lane < nz - 1, pltpu.roll(centre, nz - 1, 1), 0.0),
                    jnp.where(lane > 0, pltpu.roll(centre, 1, 1), 0.0),
                )
                steps = [centre - other for other in others]
                for k in range(terms):
                    total = factor(0, k) * steps[0]
                    for f in range(1, FACES):
                        total = total + factor(f, k) * steps[f]
                    if k == terms - 1:
                        mean[slot, pl.ds(block * PACK, PACK), :] = total
                    else:
                        place = pl.ds(k * pad + block * PACK, PACK)
                        high[place, lanes], low[place, lanes] = halves(total)

    def multiply(store, row):
        high, low, mean = store
        both = jnp.dot(table[...], high[...], preferred_element_type=jnp.float32)
        rest = jnp.dot(table[0:wide, :], low[...], preferred_element_type=jnp.float32)
        result = both[0:wide] + both[wide : 2 * wide] + rest
        for slot in range(2):
            lanes = slice(slot * nz, (slot + 1) * nz)
            for s, part in enumerate(parts):
                value = result[s * pad : (s + 1) * pad, lanes]
                if s == 0:
                    value = value + mean[slot]
                part[pl.ds(row + slot - first, mode_dev, stride=tall), :] = value[:mode_dev]

    for tile in (0, 1):
        if tile in present:
            near_in(tile).wait()
    halo_in(0, 0).wait()
    halo_in(1, 0).wait()
    build(even, first)

    def four_rows(step, carry):
        row = first + 4 * step
        multiply(even, row)
        build(odd, row + 2)
        multiply(odd, row + 2)
        build(even, jnp.minimum(row + 4, first + count - 2))
        return carry

    def tile_step(tile, carry):
        @pl.when(tile + AHEAD <= present[-1])
        def _():
            near_in(tile + AHEAD).start()

        @pl.when(tile + AHEAD - 1 < tiles)
        def _():
            start_halos(tile + AHEAD - 1)

        @pl.when(tile + 2 <= present[-1])
        def _():
            near_in(tile + 2).wait()

        @pl.when(tile + 1 < tiles)
        def _():
            halo_in(0, tile + 1).wait()
            halo_in(1, tile + 1).wait()

        lax.fori_loop(2 * tile, 2 * tile + 2, four_rows, 0)
        for s in range(groups):
            tile_out(s, tile).start()
        return carry

    lax.fori_loop(0, tiles, tile_step, 0)
    for tile in range(tiles):
        for s in range(groups):
            tile_out(s, tile).wait()


def place_sums(result, shares, shape):
    modes, _, nz = shape
    kept = [] if result is None else [result]
    steps = next(n for n in (2, 3, 1) if modes % n == 0)
    some = modes // steps
    flat = [part for _, parts in shares for part in parts]

    def kernel(*refs):
        sources = refs[len(kept) : len(kept) + len(flat)]
        out, *scratch = refs[len(kept) + len(flat) :]
        in_sems, out_sems = scratch[-2:]
        jobs, copies_out = [], []
        for step in range(steps):
            here = pl.ds(step * some, some)
            n = 0
            for (first, parts), total in zip(shares, scratch[len(flat) :]):
                copies = [
                    pltpu.make_async_copy(sources[m].at[here], scratch[m].at[here], in_sems.at[m, step])
                    for m in range(n, n + len(parts))
                ]
                for copy in copies:
                    copy.start()
                jobs.append((step, here, first, parts[0].shape[1], n, copies, total))
                n += len(parts)
        for number, (step, here, first, count, n, copies, total) in enumerate(jobs):
            for copy in copies:
                copy.wait()
            value = scratch[n][here]
            for m in range(n + 1, n + len(copies)):
                value = value + scratch[m][here]
            total[here] = value
            copies_out.append(
                pltpu.make_async_copy(total.at[here], out.at[here, pl.ds(first, count), :], out_sems.at[number])
            )
            copies_out[-1].start()
        for copy in copies_out:
            copy.wait()

    return pl.pallas_call(
        kernel,
        in_specs=[ANY] * (len(kept) + len(flat)),
        out_specs=ANY,
        out_shape=jax.ShapeDtypeStruct(shape, jnp.float32),
        scratch_shapes=[pltpu.VMEM(part.shape, jnp.float32) for part in flat]
        + [pltpu.VMEM(parts[0].shape, jnp.float32) for _, parts in shares]
        + [pltpu.SemaphoreType.DMA((len(flat), steps)), pltpu.SemaphoreType.DMA((steps * len(shares),))],
        compiler_params=pltpu.CompilerParams(vmem_limit_bytes=LIMIT),
        input_output_aliases={0: 0} if kept else {},
        name="place",
    )(*kept, *flat)


def local(mode_coeffs, mean_perm, kl_fields, couplings):
    mode_dev, _, rows, nz = mode_coeffs.shape
    terms = kl_fields.shape[0] + 1
    groups = lax.axis_size("modes")
    planes = lax.axis_size("space")
    pad = pl.cdiv(mode_dev, PACK) * PACK
    group = lax.axis_index("modes")
    pairs = [
        [pair for i in range(start, planes - 1, 2) for pair in ((i, i + 1), (i + 1, i))] for start in (1, 0)
    ]
    own3 = mode_coeffs.reshape(mode_dev, rows, nz)

    def swapped(value, side):
        return lax.ppermute(value, "space", pairs[side])

    def rotated(value, step):
        return lax.ppermute(value, "modes", [(i, (i + step) % groups) for i in range(groups)])

    def block(row_group, column_group):
        piece = lax.dynamic_slice(
            couplings,
            (0, (row_group % groups) * mode_dev, (column_group % groups) * mode_dev),
            (terms - 1, mode_dev, mode_dev),
        )
        return jnp.pad(piece, ((0, 0), (0, pad - mode_dev), (0, pad - mode_dev)))

    def split(value):
        high = lax.reduce_precision(value, 8, 7)
        return high.astype(jnp.bfloat16), (value - high).astype(jnp.bfloat16)

    quarter = pl.cdiv(pl.cdiv(rows, 4), SUB) * SUB
    gathered = [(0, quarter), (quarter, quarter + SUB)]
    begin = 2 * quarter + SUB
    half = (rows - begin) // 2 // SUB * SUB
    partial = [(begin, half), (begin + half, rows - begin - half)]

    high, low = split(jnp.concatenate([block(group, group - s) for s in range(groups)], 2))
    gathered_weights = jnp.concatenate([high, high, low], 2).reshape((terms - 1) * pad, 3 * groups * pad)
    high, low = split(jnp.concatenate([block(group + s, group) for s in range(groups)], 1))
    partial_weights = jnp.concatenate([high, low], 1)

    perm = jnp.concatenate([kl_fields, mean_perm[None]], 0).reshape(terms, rows, nz)
    perm, ready = lax.optimization_barrier((perm, own3))
    bounds = [(0, gathered[1][0] + SUB), (gathered[1][0] + SUB, gathered[1][1])]
    piece, later_piece = [ready[:, start : start + length] for start, length in bounds]
    edge = ready[:, begin:]
    perm_odd, perm_even = swapped(perm, 0), swapped(perm, 1)
    arrived = [rotated(piece, s) for s in range(1, groups)]
    edge, perm_odd, perm_even, gathered_weights, partial_weights = lax.optimization_barrier(
        (edge, perm_odd, perm_even, gathered_weights, partial_weights)
    )
    halos = [swapped(edge, 0), swapped(edge, 1)]
    later_piece, arrived = lax.optimization_barrier((later_piece, arrived))
    received = [arrived, [rotated(later_piece, s) for s in range(1, groups)]]

    params = pltpu.CompilerParams(vmem_limit_bytes=LIMIT)
    f32 = jnp.float32
    shape = (mode_dev, rows, nz)

    shares = []

    def window_scratch(count, around, inputs, outputs):
        size = count + 2 * SUB
        tiles = size // SUB
        return [
            pltpu.VMEM((3, terms, size, nz), f32),
            pltpu.SemaphoreType.DMA((3,)),
            pltpu.SemaphoreType.DMA((inputs, tiles)),
            pltpu.SemaphoreType.DMA((outputs, tiles)),
            pltpu.VMEM((FACES * terms * (count + around * SUB), nz), f32),
        ]

    def window_modes(count):
        return mode_dev, spaced(count + 2 * SUB), nz

    def cost(count):
        products = 3 * 2 * (terms - 1) * mode_dev * mode_dev * groups * count * nz
        return pl.CostEstimate(flops=products // 1024, bytes_accessed=2**10 * count, transcendentals=0)

    def partial_shares(index, source):
        first, count = partial[index]
        flat = jax.ShapeDtypeStruct((mode_dev, count, nz), f32)
        outs = pl.pallas_call(
            functools.partial(partial_kernel, first, count, rows, mode_dev, pad, groups, partial[0][0]),
            in_specs=[HBM] * 6 + [VMEM],
            out_specs=[HBM] * groups,
            out_shape=[flat] * groups,
            scratch_shapes=[pltpu.VMEM(window_modes(count), f32), pltpu.VMEM((2, mode_dev, spaced(count), nz), f32)]
            + window_scratch(count, 0, 3, groups)
            + [
                pltpu.VMEM(((terms - 1) * pad, 2 * nz), jnp.bfloat16),
                pltpu.VMEM(((terms - 1) * pad, 2 * nz), jnp.bfloat16),
                pltpu.VMEM((2, pad, nz), f32),
            ]
            * 2
            + [
                pltpu.VMEM((groups, mode_dev, spaced(count), nz), f32),
                pltpu.VMEM((2 * groups * pad, (terms - 1) * pad), jnp.bfloat16),
            ],
            compiler_params=params,
            cost_estimate=cost(count),
            name="partial",
        )(source, *halos, perm, perm_odd, perm_even, partial_weights)
        parts = [outs[0]] + [rotated(value, s) for s, value in enumerate(outs[1:], 1)]
        return first, parts

    def gathered_shares(index, source):
        first, count = gathered[index]
        sources = bounds[: index + 1]
        pieces = [piece for group_pieces in received[: index + 1] for piece in group_pieces]
        flat = jax.ShapeDtypeStruct((mode_dev, count, nz), f32)
        centre, to_odd, to_even = pl.pallas_call(
            functools.partial(
                gathered_kernel, first, count, rows, mode_dev, pad, groups, sources
            ),
            in_specs=[HBM] * 4 + [VMEM] + [HBM] * len(pieces),
            out_specs=[HBM] * 3,
            out_shape=[flat] * 3,
            scratch_shapes=[pltpu.VMEM(window_modes(count), f32), pltpu.VMEM((groups - 1, *window_modes(count)), f32)]
            + window_scratch(count, 1, groups, 3)
            + [
                pltpu.VMEM((3 * groups * pad, 2 * nz), jnp.bfloat16),
                pltpu.VMEM(((terms - 1) * pad, 2 * nz), f32),
            ]
            * 2
            + [pltpu.VMEM((pad, nz), f32)] * 2
            + [pltpu.VMEM(window_modes(count), f32)] * 3,
            compiler_params=params,
            cost_estimate=cost(count),
            name="gathered",
        )(source, perm, perm_odd, perm_even, gathered_weights, *pieces)
        if index == 0:
            to_odd, to_even, *halos[:] = lax.optimization_barrier((to_odd, to_even, *halos))
        parts = [centre, swapped(to_odd, 0), swapped(to_even, 1)]
        return first, parts

    shares, source = [], own3
    for compute, index in ((gathered_shares, 0), (partial_shares, 0), (gathered_shares, 1), (partial_shares, 1)):
        if len(shares) == 3:
            source, shares[0][1][1:], shares[1][1][1:] = lax.optimization_barrier(
                (source, shares[0][1][1:], shares[1][1][1:])
            )
        share = compute(index, source)
        source, share[1][0] = lax.optimization_barrier((source, share[1][0]))
        shares.append(share)
    result = place_sums(None, shares[:2], shape)
    result = place_sums(result, shares[2:], shape)
    return result.reshape(mode_coeffs.shape)


def solution(mesh):
    in_specs = (
        P("modes", "space", None, None),
        P("space", None, None),
        P(None, "space", None, None),
        P(),
    )
    out_specs = P("modes", "space", None, None)
    return jax.shard_map(local, mesh=mesh, in_specs=in_specs, out_specs=out_specs, check_vma=False)
```

```python
import functools

import jax
import jax.numpy as jnp
from jax import lax
from jax.experimental import pallas as pl
from jax.experimental.pallas import tpu as pltpu
from jax.sharding import PartitionSpec as P

SUB = 8
AHEAD = 3
PACK = 16
FACES = 6
LIMIT = 48 * 2**20
VMEM = pl.BlockSpec(memory_space=pltpu.VMEM)
ANY = pl.BlockSpec(memory_space=pl.ANY)
HBM = pl.BlockSpec(memory_space=pltpu.HBM)


def halves(value):
    high = value.astype(jnp.bfloat16)
    low = (value - high.astype(jnp.float32)).astype(jnp.bfloat16)
    return high, low


def spaced(count):
    return count + SUB if count // SUB % 2 == 0 else count


def tile_copy(source, row, target, at, semaphore):
    return pltpu.make_async_copy(
        source.at[:, pl.ds(pl.multiple_of(row, SUB), SUB), :],
        target.at[:, pl.ds(pl.multiple_of(at, SUB), SUB), :],
        semaphore,
    )


def window_fields(perms, fields, first, count, rows, semaphores):
    begin, end = max(first - SUB, 0), min(first + count + SUB, rows)
    there = pl.ds(begin - first + SUB, end - begin)
    copies = []
    for n, ref in enumerate(perms):
        copies.append(
            pltpu.make_async_copy(ref.at[:, pl.ds(begin, end - begin), :], fields.at[n, :, there, :], semaphores.at[n])
        )
    for copy in copies:
        copy.start()
    return copies


def clear_outside(first, count, rows, fields, windows):
    for outside, at in ((first == 0, 0), (first + count == rows, count + SUB)):
        if outside:
            tile = pl.ds(at, SUB)
            fields[0, :, tile, :] = jnp.zeros((fields.shape[1], SUB, fields.shape[3]), fields.dtype)
            for ref in windows:
                ref[:, tile, :] = jnp.zeros((ref.shape[0], SUB, ref.shape[2]), ref.dtype)


def face_coefs(coef, fields, begin, count):
    terms, nz = fields.shape[1], fields.shape[3]
    span = coef.shape[0] // (FACES * terms)
    lane = lax.broadcasted_iota(jnp.int32, (count, nz), 1)
    for k in range(terms):
        here = fields[0, k, pl.ds(begin, count), :]
        others = (
            fields[1, k, pl.ds(begin, count), :],
            fields[2, k, pl.ds(begin, count), :],
            fields[0, k, pl.ds(begin + 1, count), :],
            fields[0, k, pl.ds(begin - 1, count), :],
            jnp.where(lane < nz - 1, pltpu.roll(here, nz - 1, 1), 0.0),
            jnp.where(lane > 0, pltpu.roll(here, 1, 1), 0.0),
        )
        for f, other in enumerate(others):
            coef[pl.ds((f * terms + k) * span, count), :] = 0.5 * (here + other)


def strided_rows(ref, start, count, stride):
    return ref[pl.ds(start, count, stride=stride), :]


def mode_block(ref, block, row, modes, stride):
    size = min(PACK, modes - block * PACK)
    value = strided_rows(ref, block * PACK * stride + row, size, stride)
    if size == PACK:
        return value
    return jnp.concatenate([value, jnp.zeros((PACK - size, value.shape[1]), value.dtype)], 0)


def factor_of(coef, at, terms, span):
    def factor(f, k):
        value = coef[pl.ds((f * terms + k) * span + at, SUB, stride=0), :]
        return jnp.concatenate([value] * (PACK // SUB), 0)

    return factor


def gathered_kernel(first, count, rows, mode_dev, pad, groups, sources, *refs):
    own_all, perm, perm_odd, perm_even, weights = refs[:5]
    pieces = refs[5 : 5 + len(sources) * (groups - 1)]
    results = refs[5 + len(pieces) : 8 + len(pieces)]
    near, far, fields, field_sems, in_sems, out_sems, coef = refs[8 + len(pieces) : 15 + len(pieces)]
    stack_even, mixed_even, stack_odd, mixed_odd, pending, above, *parts = refs[15 + len(pieces) :]
    terms, nz = fields.shape[1], fields.shape[3]
    span = coef.shape[0] // (FACES * terms)
    base, size = first - SUB, near.shape[1]
    tiles = count // SUB
    windows = [near] + [far.at[s] for s in range(groups - 1)]

    def tile_in(s, tile, index):
        row = base + tile * SUB
        if s == 0:
            return tile_copy(own_all, row, windows[0], tile * SUB, in_sems.at[0, tile])
        piece = pieces[index * (groups - 1) + s - 1]
        return tile_copy(piece, row - sources[index][0], windows[s], tile * SUB, in_sems.at[s, tile])

    def tile_out(n, tile):
        return tile_copy(parts[n], (tile + 1) * SUB, results[n], tile * SUB, out_sems.at[n, tile])

    field_copies = window_fields((perm, perm_odd, perm_even), fields, first, count, rows, field_sems)
    present = [tile for tile in range(tiles + 2) if 0 <= base + tile * SUB < rows]
    latest = len(sources) - 1
    early = {tile: max(latest - 1, 0) if tile < 2 else latest for tile in present}
    def start_in(tile, index):
        for s in range(groups):
            tile_in(s, tile, index).start()

    for tile in present:
        if tile < AHEAD:
            start_in(tile, early[tile])
    clear_outside(first, count, rows, fields, windows)
    for copy in field_copies:
        copy.wait()
    own, *others = [ref.reshape(mode_dev * size, nz) for ref in windows]
    tall = parts[0].shape[1]
    out, to_odd, to_even = [part.reshape(mode_dev * tall, nz) for part in parts]
    face_coefs(coef, fields, SUB - 1, span)
    pending[...] = jnp.zeros_like(pending)
    above[...] = jnp.zeros_like(above)
    lane = lax.broadcasted_iota(jnp.int32, (PACK, nz), 1)
    wide = groups * pad
    blocks = [(block, min(PACK, mode_dev - block * PACK)) for block in range(pad // PACK)]

    def mix(stack, mixed, row):
        for slot in range(2):
            lanes = pl.ds(slot * nz, nz)
            for s, piece in enumerate([own, *others]):
                for block, _ in blocks:
                    high, low = halves(mode_block(piece, block, row + slot - base, mode_dev, size))
                    place = s * pad + block * PACK
                    stack[place : place + PACK, lanes] = high
                    stack[wide + place : wide + place + PACK, lanes] = low
        mixed[...] = jnp.dot(weights[...], stack[...], preferred_element_type=jnp.float32)

    def spread(mixed, row):
        for block, modes in blocks:
            here = pl.ds(block * PACK, PACK)
            for slot in range(2):
                factor = factor_of(coef, row + slot - first + 1, terms, span)
                totals = [None] * FACES
                for k in range(terms):
                    if k == terms - 1:
                        value = mode_block(own, block, row + slot - base, mode_dev, size)
                    else:
                        lanes, at = pl.ds(slot * nz, nz), k * pad + block * PACK
                        value = mixed[pl.ds(at, PACK), lanes] + mixed[pl.ds(at + (terms - 1) * pad, PACK), lanes]
                    for f in range(FACES):
                        part = factor(f, k) * value
                        totals[f] = part if totals[f] is None else totals[f] + part
                odd, even, north, south, east, west = totals
                at = block * PACK * tall + row + slot - first + SUB
                place = pl.ds(at, modes, stride=tall)
                to_odd[place, :] = -odd[:modes]
                to_even[place, :] = -even[:modes]
                moved_east = jnp.where(lane > 0, pltpu.roll(east, 1, 1), 0.0)
                moved_west = jnp.where(lane < nz - 1, pltpu.roll(west, nz - 1, 1), 0.0)
                total = ((odd + even) + (north + south)) + ((east - moved_east) + (west - moved_west))
                back = pl.ds(at - 1, modes, stride=tall)
                if slot == 0:
                    out[back, :] = (pending[here, :] - south)[:modes]
                    carried = total - above[here, :], north
                else:
                    out[back, :] = (carried[0] - south)[:modes]
                    pending[here, :] = total - carried[1]
                    above[here, :] = north

    def wait_in(tile, index):
        for s in range(groups):
            tile_in(s, tile, index).wait()

    for tile in (0, 1):
        if tile in present:
            wait_in(tile, early[tile])
    mix(stack_even, mixed_even, first - 1)

    def four_rows(step, carry):
        row = first - 1 + 4 * step
        mix(stack_odd, mixed_odd, row + 2)
        spread(mixed_even, row)
        mix(stack_even, mixed_even, row + 4)
        spread(mixed_odd, row + 2)
        return carry

    def tile_step(tile, carry):
        @pl.when(tile + AHEAD <= present[-1])
        def _():
            start_in(tile + AHEAD, latest)

        @pl.when(tile + 2 <= present[-1])
        def _():
            wait_in(tile + 2, latest)

        lax.fori_loop(2 * tile, 2 * tile + 2, four_rows, 0)

        @pl.when(tile > 0)
        def _():
            for n in range(3):
                tile_out(n, tile - 1).start()

        return carry

    lax.fori_loop(0, tiles, tile_step, 0)
    spread(mixed_even, first - 1 + count)
    for n in range(3):
        tile_out(n, tiles - 1).start()
    for tile in range(tiles):
        for n in range(3):
            tile_out(n, tile).wait()


def partial_kernel(first, count, rows, mode_dev, pad, groups, halo_first, *refs):
    own_all, odd_all, even_all, perm, perm_odd, perm_even, weights = refs[:7]
    results = refs[7 : 7 + groups]
    near, halo, fields, field_sems, in_sems, out_sems, coef, high_even, low_even, mean_even, high_odd, low_odd, mean_odd, shares, table = refs[7 + groups :]
    even, odd = (high_even, low_even, mean_even), (high_odd, low_odd, mean_odd)
    terms, nz = fields.shape[1], fields.shape[3]
    base, size = first - SUB, near.shape[1]
    tall = halo.shape[2]
    tiles = count // SUB

    def near_in(tile):
        return tile_copy(own_all, base + tile * SUB, near, tile * SUB, in_sems.at[0, tile])

    def halo_in(side, tile):
        ref = (odd_all, even_all)[side]
        return tile_copy(ref, first - halo_first + tile * SUB, halo.at[side], tile * SUB, in_sems.at[1 + side, tile])

    def tile_out(s, tile):
        return tile_copy(shares.at[s], tile * SUB, results[s], tile * SUB, out_sems.at[s, tile])

    field_copies = window_fields((perm, perm_odd, perm_even), fields, first, count, rows, field_sems)
    present = [tile for tile in range(tiles + 2) if 0 <= base + tile * SUB < rows]
    def start_halos(tile):
        halo_in(0, tile).start()
        halo_in(1, tile).start()

    for tile in range(AHEAD):
        if tile in present:
            near_in(tile).start()
        if tile < min(AHEAD - 1, tiles):
            start_halos(tile)
    clear_outside(first, count, rows, fields, [near])
    for k in range(weights.shape[0]):
        table[:, k * pad : (k + 1) * pad] = weights[k]
    for copy in field_copies:
        copy.wait()
    own = near.reshape(mode_dev * size, nz)
    side_odd, side_even = halo.at[0].reshape(mode_dev * tall, nz), halo.at[1].reshape(mode_dev * tall, nz)
    parts = [shares.at[s].reshape(mode_dev * tall, nz) for s in range(groups)]
    face_coefs(coef, fields, SUB, count)
    lane = lax.broadcasted_iota(jnp.int32, (PACK, nz), 1)
    wide = groups * pad

    def build(store, row):
        high, low, mean = store
        for slot in range(2):
            lanes = pl.ds(slot * nz, nz)
            at = row + slot
            factor = factor_of(coef, at - first, terms, count)
            for block in range(pad // PACK):
                centre = mode_block(own, block, at - base, mode_dev, size)
                others = (
                    mode_block(side_odd, block, at - first, mode_dev, tall),
                    mode_block(side_even, block, at - first, mode_dev, tall),
                    mode_block(own, block, at + 1 - base, mode_dev, size),
                    mode_block(own, block, at - 1 - base, mode_dev, size),
                    jnp.where(lane < nz - 1, pltpu.roll(centre, nz - 1, 1), 0.0),
                    jnp.where(lane > 0, pltpu.roll(centre, 1, 1), 0.0),
                )
                steps = [centre - other for other in others]
                for k in range(terms):
                    total = factor(0, k) * steps[0]
                    for f in range(1, FACES):
                        total = total + factor(f, k) * steps[f]
                    if k == terms - 1:
                        mean[slot, pl.ds(block * PACK, PACK), :] = total
                    else:
                        place = pl.ds(k * pad + block * PACK, PACK)
                        high[place, lanes], low[place, lanes] = halves(total)

    def multiply(store, row):
        high, low, mean = store
        both = jnp.dot(table[...], high[...], preferred_element_type=jnp.float32)
        rest = jnp.dot(table[0:wide, :], low[...], preferred_element_type=jnp.float32)
        result = both[0:wide] + both[wide : 2 * wide] + rest
        for slot in range(2):
            lanes = slice(slot * nz, (slot + 1) * nz)
            for s, part in enumerate(parts):
                value = result[s * pad : (s + 1) * pad, lanes]
                if s == 0:
                    value = value + mean[slot]
                part[pl.ds(row + slot - first, mode_dev, stride=tall), :] = value[:mode_dev]

    for tile in (0, 1):
        if tile in present:
            near_in(tile).wait()
    halo_in(0, 0).wait()
    halo_in(1, 0).wait()
    build(even, first)

    def four_rows(step, carry):
        row = first + 4 * step
        multiply(even, row)
        build(odd, row + 2)
        multiply(odd, row + 2)
        build(even, jnp.minimum(row + 4, first + count - 2))
        return carry

    def tile_step(tile, carry):
        @pl.when(tile + AHEAD <= present[-1])
        def _():
            near_in(tile + AHEAD).start()

        @pl.when(tile + AHEAD - 1 < tiles)
        def _():
            start_halos(tile + AHEAD - 1)

        @pl.when(tile + 2 <= present[-1])
        def _():
            near_in(tile + 2).wait()

        @pl.when(tile + 1 < tiles)
        def _():
            halo_in(0, tile + 1).wait()
            halo_in(1, tile + 1).wait()

        lax.fori_loop(2 * tile, 2 * tile + 2, four_rows, 0)
        for s in range(groups):
            tile_out(s, tile).start()
        return carry

    lax.fori_loop(0, tiles, tile_step, 0)
    for tile in range(tiles):
        for s in range(groups):
            tile_out(s, tile).wait()


def place_sums(result, shares, shape):
    modes, _, nz = shape
    kept = [] if result is None else [result]
    steps = next(n for n in (2, 3, 1) if modes % n == 0)
    some = modes // steps
    flat = [part for _, parts in shares for part in parts]

    def kernel(*refs):
        sources = refs[len(kept) : len(kept) + len(flat)]
        out, *scratch = refs[len(kept) + len(flat) :]
        in_sems, out_sems = scratch[-2:]
        jobs, copies_out = [], []
        for step in range(steps):
            here = pl.ds(step * some, some)
            n = 0
            for (first, parts), total in zip(shares, scratch[len(flat) :]):
                copies = [
                    pltpu.make_async_copy(sources[m].at[here], scratch[m].at[here], in_sems.at[m, step])
                    for m in range(n, n + len(parts))
                ]
                for copy in copies:
                    copy.start()
                jobs.append((step, here, first, parts[0].shape[1], n, copies, total))
                n += len(parts)
        for number, (step, here, first, count, n, copies, total) in enumerate(jobs):
            for copy in copies:
                copy.wait()
            value = scratch[n][here]
            for m in range(n + 1, n + len(copies)):
                value = value + scratch[m][here]
            total[here] = value
            copies_out.append(
                pltpu.make_async_copy(total.at[here], out.at[here, pl.ds(first, count), :], out_sems.at[number])
            )
            copies_out[-1].start()
        for copy in copies_out:
            copy.wait()

    return pl.pallas_call(
        kernel,
        in_specs=[ANY] * (len(kept) + len(flat)),
        out_specs=ANY,
        out_shape=jax.ShapeDtypeStruct(shape, jnp.float32),
        scratch_shapes=[pltpu.VMEM(part.shape, jnp.float32) for part in flat]
        + [pltpu.VMEM(parts[0].shape, jnp.float32) for _, parts in shares]
        + [pltpu.SemaphoreType.DMA((len(flat), steps)), pltpu.SemaphoreType.DMA((steps * len(shares),))],
        compiler_params=pltpu.CompilerParams(vmem_limit_bytes=LIMIT),
        input_output_aliases={0: 0} if kept else {},
        name="place",
    )(*kept, *flat)


def local(mode_coeffs, mean_perm, kl_fields, couplings):
    mode_dev, _, rows, nz = mode_coeffs.shape
    terms = kl_fields.shape[0] + 1
    groups = lax.axis_size("modes")
    planes = lax.axis_size("space")
    pad = pl.cdiv(mode_dev, PACK) * PACK
    group = lax.axis_index("modes")
    pairs = [
        [pair for i in range(start, planes - 1, 2) for pair in ((i, i + 1), (i + 1, i))] for start in (1, 0)
    ]
    own3 = mode_coeffs.reshape(mode_dev, rows, nz)

    def swapped(value, side):
        return lax.ppermute(value, "space", pairs[side])

    def rotated(value, step):
        return lax.ppermute(value, "modes", [(i, (i + step) % groups) for i in range(groups)])

    def block(row_group, column_group):
        piece = lax.dynamic_slice(
            couplings,
            (0, (row_group % groups) * mode_dev, (column_group % groups) * mode_dev),
            (terms - 1, mode_dev, mode_dev),
        )
        return jnp.pad(piece, ((0, 0), (0, pad - mode_dev), (0, pad - mode_dev)))

    def split(value):
        high = lax.reduce_precision(value, 8, 7)
        return high.astype(jnp.bfloat16), (value - high).astype(jnp.bfloat16)

    quarter = pl.cdiv(pl.cdiv(rows, 4), SUB) * SUB
    gathered = [(0, quarter), (quarter, quarter + SUB)]
    begin = 2 * quarter + SUB
    half = (rows - begin) // 2 // SUB * SUB
    partial = [(begin, half), (begin + half, rows - begin - half)]

    high, low = split(jnp.concatenate([block(group, group - s) for s in range(groups)], 2))
    gathered_weights = jnp.concatenate(
        [
            jnp.concatenate(pair, 2).reshape((terms - 1) * pad, 2 * groups * pad)
            for pair in ((high, high), (low, jnp.zeros_like(low)))
        ],
        0,
    )
    high, low = split(jnp.concatenate([block(group + s, group) for s in range(groups)], 1))
    partial_weights = jnp.concatenate([high, low], 1)

    perm = jnp.concatenate([kl_fields, mean_perm[None]], 0).reshape(terms, rows, nz)
    perm, ready = lax.optimization_barrier((perm, own3))
    bounds = [(0, gathered[1][0] + SUB), (gathered[1][0] + SUB, gathered[1][1])]
    piece, later_piece = [ready[:, start : start + length] for start, length in bounds]
    edge = ready[:, begin:]
    perm_odd, perm_even = swapped(perm, 0), swapped(perm, 1)
    arrived = [rotated(piece, s) for s in range(1, groups)]
    edge, perm_odd, perm_even, gathered_weights, partial_weights = lax.optimization_barrier(
        (edge, perm_odd, perm_even, gathered_weights, partial_weights)
    )
    halos = [swapped(edge, 0), swapped(edge, 1)]
    later_piece, arrived = lax.optimization_barrier((later_piece, arrived))
    received = [arrived, [rotated(later_piece, s) for s in range(1, groups)]]

    params = pltpu.CompilerParams(vmem_limit_bytes=LIMIT)
    f32 = jnp.float32
    shape = (mode_dev, rows, nz)

    shares = []

    def window_scratch(count, around, inputs, outputs):
        size = count + 2 * SUB
        tiles = size // SUB
        return [
            pltpu.VMEM((3, terms, size, nz), f32),
            pltpu.SemaphoreType.DMA((3,)),
            pltpu.SemaphoreType.DMA((inputs, tiles)),
            pltpu.SemaphoreType.DMA((outputs, tiles)),
            pltpu.VMEM((FACES * terms * (count + around * SUB), nz), f32),
        ]

    def window_modes(count):
        return mode_dev, spaced(count + 2 * SUB), nz

    def cost(count):
        products = 3 * 2 * (terms - 1) * mode_dev * mode_dev * groups * count * nz
        return pl.CostEstimate(flops=products // 1024, bytes_accessed=2**10 * count, transcendentals=0)

    def partial_shares(index, source):
        first, count = partial[index]
        flat = jax.ShapeDtypeStruct((mode_dev, count, nz), f32)
        outs = pl.pallas_call(
            functools.partial(partial_kernel, first, count, rows, mode_dev, pad, groups, partial[0][0]),
            in_specs=[HBM] * 6 + [VMEM],
            out_specs=[HBM] * groups,
            out_shape=[flat] * groups,
            scratch_shapes=[pltpu.VMEM(window_modes(count), f32), pltpu.VMEM((2, mode_dev, spaced(count), nz), f32)]
            + window_scratch(count, 0, 3, groups)
            + [
                pltpu.VMEM(((terms - 1) * pad, 2 * nz), jnp.bfloat16),
                pltpu.VMEM(((terms - 1) * pad, 2 * nz), jnp.bfloat16),
                pltpu.VMEM((2, pad, nz), f32),
            ]
            * 2
            + [
                pltpu.VMEM((groups, mode_dev, spaced(count), nz), f32),
                pltpu.VMEM((2 * groups * pad, (terms - 1) * pad), jnp.bfloat16),
            ],
            compiler_params=params,
            cost_estimate=cost(count),
            name="partial",
        )(source, *halos, perm, perm_odd, perm_even, partial_weights)
        parts = [outs[0]] + [rotated(value, s) for s, value in enumerate(outs[1:], 1)]
        return first, parts

    def gathered_shares(index, source):
        first, count = gathered[index]
        sources = bounds[: index + 1]
        pieces = [piece for group_pieces in received[: index + 1] for piece in group_pieces]
        flat = jax.ShapeDtypeStruct((mode_dev, count, nz), f32)
        centre, to_odd, to_even = pl.pallas_call(
            functools.partial(
                gathered_kernel, first, count, rows, mode_dev, pad, groups, sources
            ),
            in_specs=[HBM] * 4 + [VMEM] + [HBM] * len(pieces),
            out_specs=[HBM] * 3,
            out_shape=[flat] * 3,
            scratch_shapes=[pltpu.VMEM(window_modes(count), f32), pltpu.VMEM((groups - 1, *window_modes(count)), f32)]
            + window_scratch(count, 1, groups, 3)
            + [
                pltpu.VMEM((2 * groups * pad, 2 * nz), jnp.bfloat16),
                pltpu.VMEM((2 * (terms - 1) * pad, 2 * nz), f32),
            ]
            * 2
            + [pltpu.VMEM((pad, nz), f32)] * 2
            + [pltpu.VMEM(window_modes(count), f32)] * 3,
            compiler_params=params,
            cost_estimate=cost(count),
            name="gathered",
        )(source, perm, perm_odd, perm_even, gathered_weights, *pieces)
        if index == 0:
            to_odd, to_even, *halos[:] = lax.optimization_barrier((to_odd, to_even, *halos))
        parts = [centre, swapped(to_odd, 0), swapped(to_even, 1)]
        return first, parts

    shares, source = [], own3
    for compute, index in ((gathered_shares, 0), (partial_shares, 0), (gathered_shares, 1), (partial_shares, 1)):
        if len(shares) == 3:
            source, shares[0][1][1:], shares[1][1][1:] = lax.optimization_barrier(
                (source, shares[0][1][1:], shares[1][1][1:])
            )
        share = compute(index, source)
        source, share[1][0] = lax.optimization_barrier((source, share[1][0]))
        shares.append(share)
    result = place_sums(None, shares[:2], shape)
    result = place_sums(result, shares[2:], shape)
    return result.reshape(mode_coeffs.shape)


def solution(mesh):
    in_specs = (
        P("modes", "space", None, None),
        P("space", None, None),
        P(None, "space", None, None),
        P(),
    )
    out_specs = P("modes", "space", None, None)
    return jax.shard_map(local, mesh=mesh, in_specs=in_specs, out_specs=out_specs, check_vma=False)
```
